32 devices in a mesh: rep: 4 (over x, core), tile: 8 (over z, y).
Axes of the slice: x: 2, y: 2, z: 4, core: 2. Of those that a mesh axis runs over, the one named last changes fastest.
Arguments:
- fields: bfloat16 [4, 192, 8, 8, 256], P('rep', 'tile'), may hold values from -6 to 6
- cotangent: bfloat16 [4, 192, 8, 8, 256], P('rep', 'tile'), may hold values from -6 to 6
- weights: float32 [4, 2304, 256], P('rep', 'tile'), may hold values from -6 to 6
- ema: float32 [4, 2304, 256], P('rep', 'tile'), may hold values from -6 to 6
- tile_links: int32 [192, 4], replicated, may hold values from 0 to 191, as said below
- tile_codes: int32 [192, 4], replicated, may hold values from 0 to 3
- corner_links: int32 [192, 4], replicated, may hold values from -1 to 191, as said below
- corner_codes: int32 [192, 4], replicated, may hold values from 0 to 3
- gossip_bit: int32 [1], replicated, may hold values from 0 to 1
- batch_size: int32 [1], replicated, may hold values from 32 to 512
Outputs:
- activations: bfloat16 [4, 192, 8, 8, 256], P('rep', 'tile')
- field_grad: bfloat16 [4, 192, 8, 8, 256], P('rep', 'tile')
- averaged: float32 [4, 2304, 256], P('rep', 'tile')
- ema_out: float32 [4, 2304, 256], P('rep', 'tile')
The draws below stay inside these ranges and needn't reach their ends.
Inputs may be any that keep to these rules, and one draw needn't show every extreme that they name: tile_links, tile_codes, corner_links and corner_codes describe the tiles of a HEALPix sphere: 12 base faces, each cut into 4 x 4 tiles, numbered face by face (the order of the faces drawn from the seed) and row by row within a face. The relation is symmetric: if tile u lies across edge q of tile t as its edge e, then t lies across edge e of u as its edge q, and cells along a shared edge run in the same order on both tiles; likewise, if corner q of t takes corner cell c of u, then corner c of u takes corner cell q of t. `corner_links`: -1 exactly at the tiles' corners that touch one of the 8 vertices where only three base faces meet.
All inputs are finite; a program needn't handle non-finite values.
Results may differ from the reference program's by a relative error of at most 0.0014.
The reference program's roundings to bfloat16 on the way count: a program that leaves them out, or rounds other values in their place, can miss the bound.
Values may be sent and summed in bfloat16 or wider, within the bound.
A program may use at most 64 MiB of HBM per device.

```python
import jax
import jax.numpy as jnp
import numpy as np
from jax import lax

C = 256
SUB = 4
TS = 8
TILES = 192
REPS = 4
KROWS = 2304


def face_id(cycle_index, column):
    return cycle_index * 4 + column % 4


def face_cell(face, pos_x, pos_y, span):
    cycle_index = face // 4
    column = face % 4
    last = span - 1
    inside_x = 0 <= pos_x <= last
    inside_y = 0 <= pos_y <= last
    if inside_x and inside_y:
        return (face, pos_x, pos_y)
    if not inside_x and (not inside_y):
        if pos_x > last and pos_y > last:
            if cycle_index == 0:
                return (face_id(0, column + 2), last, last)
            if cycle_index == 2:
                return (face_id(0, column), 0, 0)
            return None
        if pos_x < 0 and pos_y < 0:
            if cycle_index == 0:
                return (face_id(2, column), last, last)
            if cycle_index == 2:
                return (face_id(2, column + 2), 0, 0)
            return None
        if pos_x > last and pos_y < 0:
            if cycle_index == 1:
                return (face_id(1, column + 1), 0, last)
            return None
        if cycle_index == 1:
            return (face_id(1, column - 1), last, 0)
        return None
    if cycle_index == 0:
        if pos_x > last:
            return (face_id(0, column + 1), pos_y, last)
        if pos_y > last:
            return (face_id(0, column - 1), last, pos_x)
        if pos_x < 0:
            return (face_id(1, column), last, pos_y)
        return (face_id(1, column + 1), pos_x, last)
    if cycle_index == 1:
        if pos_x > last:
            return (face_id(0, column), 0, pos_y)
        if pos_y > last:
            return (face_id(0, column - 1), pos_x, 0)
        if pos_x < 0:
            return (face_id(2, column - 1), last, pos_y)
        return (face_id(2, column), pos_x, last)
    if pos_x > last:
        return (face_id(1, column + 1), 0, pos_y)
    if pos_y > last:
        return (face_id(1, column), pos_x, 0)
    if pos_x < 0:
        return (face_id(2, column - 1), pos_y, 0)
    return (face_id(2, column + 1), 0, pos_x)


def sphere_tables():
    tile_side = 4
    span = SUB * tile_side
    per_face = SUB * SUB
    total_tiles = 12 * per_face
    link_table = np.zeros((total_tiles, 4), np.int32)
    code_table = np.zeros((total_tiles, 4), np.int32)
    corner_table = np.zeros((total_tiles, 4), np.int32)
    corner_code_table = np.zeros((total_tiles, 4), np.int32)
    corner_offsets = [(-1, -1), (-1, tile_side), (tile_side, -1), (tile_side, tile_side)]
    for face in range(12):
        for row_block in range(SUB):
            for col_block in range(SUB):
                tile_id = face * per_face + row_block * SUB + col_block
                base_x = row_block * tile_side
                base_y = col_block * tile_side
                for side_id in range(4):
                    found = []
                    for along in range(2):
                        offset = [(-1, along), (tile_side, along), (along, -1), (along, tile_side)][side_id]
                        found.append(face_cell(face, base_x + offset[0], base_y + offset[1], span))
                    other_face, cell_x, cell_y = found[0]
                    link_table[tile_id, side_id] = other_face * per_face + cell_x // tile_side * SUB + cell_y // tile_side
                    local_x = cell_x % tile_side
                    local_y = cell_y % tile_side
                    if found[1][1] == cell_x:
                        code_table[tile_id, side_id] = 0 if local_x == 0 else 1
                    else:
                        code_table[tile_id, side_id] = 2 if local_y == 0 else 3
                for corner_id in range(4):
                    offset = corner_offsets[corner_id]
                    across = face_cell(face, base_x + offset[0], base_y + offset[1], span)
                    if across is None:
                        corner_table[tile_id, corner_id] = -1
                        corner_code_table[tile_id, corner_id] = 0
                    else:
                        other_face, cell_x, cell_y = across
                        corner_table[tile_id, corner_id] = other_face * per_face + cell_x // tile_side * SUB + cell_y // tile_side
                        corner_code_table[tile_id, corner_id] = 2 * int(cell_x % tile_side == tile_side - 1) + int(cell_y % tile_side == tile_side - 1)
    return (link_table, code_table, corner_table, corner_code_table)


def sphere_draw(key):
    link_table, code_table, corner_table, corner_code_table = sphere_tables()
    per_face = SUB * SUB
    column = jax.random.randint(jax.random.fold_in(key, 11), (), 0, 4).astype(jnp.int32)
    first_face = 8 + column
    second_face = 8 + (column + 3) % 4
    face_ids = jnp.arange(12, dtype=jnp.int32)
    scores = jax.random.permutation(jax.random.fold_in(key, 12), 12).astype(jnp.int32)
    scores = jnp.where(face_ids == first_face, 100, jnp.where(face_ids == second_face, 101, scores))
    ranked = jnp.argsort(scores, stable=True).astype(jnp.int32)
    face_at_pos = jnp.concatenate([ranked[10:11], ranked[0:5], ranked[11:12], ranked[5:10]])
    pos_of = jnp.zeros((12,), jnp.int32).at[face_at_pos].set(face_ids)
    tile_ids = jnp.arange(12 * per_face, dtype=jnp.int32)
    faces = tile_ids // per_face
    renamed = pos_of[faces] * per_face + tile_ids % per_face
    empty = jnp.zeros((12 * per_face, 4), jnp.int32)
    links = empty.at[renamed].set(renamed[jnp.asarray(link_table)])
    codes = empty.at[renamed].set(jnp.asarray(code_table))
    corner_base = jnp.asarray(corner_table)
    corner_named = jnp.where(corner_base >= 0, renamed[jnp.maximum(corner_base, 0)], -1)
    corners = empty.at[renamed].set(corner_named)
    corner_codes = empty.at[renamed].set(jnp.asarray(corner_code_table))
    return (links, codes, corners, corner_codes)


def draw_tile_links(key, part):
    return sphere_draw(key)[0]


def draw_tile_codes(key, part):
    return sphere_draw(key)[1]


def draw_corner_links(key, part):
    return sphere_draw(key)[2]


def draw_corner_codes(key, part):
    return sphere_draw(key)[3]


def shard_levels(key, extent, shards, low, high):
    gain = 1.0
    for position, shards_of in shards:
        draws = jax.random.uniform(jax.random.fold_in(jax.random.fold_in(key, 6), position), (shards_of,), jnp.float32, low / len(shards), high / len(shards))
        gain = gain * jnp.repeat(jnp.exp(draws), extent[position] // shards_of).reshape((-1,) + (1,) * (len(extent) - 1 - position))
    return gain


def centred(own_key, dims, width, reach, cuts=(), held_as=jnp.bfloat16):
    entries = jax.random.normal(own_key, dims, jnp.float32) * width
    if len(cuts) > 0:
        entries = shard_levels(own_key, dims, cuts, -0.22, 0.18) * entries
    return jnp.clip(entries, min=-reach, max=reach).astype(held_as)


def setup_inputs(seed: int = 0) -> dict:
    key_of = jax.random.split(jax.random.key(seed), 11)
    fields = centred(key_of[0], (REPS, TILES, TS, TS, C), 1.0, 6.0, ((0, 4), (1, 8)))
    cotangent = centred(key_of[1], (REPS, TILES, TS, TS, C), 1.0, 6.0, ((0, 4), (1, 8)))
    weights = centred(key_of[2], (REPS, KROWS, C), 1.0, 6.0, ((0, 4), (1, 8)), jnp.float32)
    ema = centred(key_of[3], (REPS, KROWS, C), 1.0, 6.0, ((0, 4), (1, 8)), jnp.float32)
    tile_links = draw_tile_links(jax.random.fold_in(key_of[10], 71), 0)
    tile_codes = draw_tile_codes(jax.random.fold_in(key_of[10], 71), 0)
    corner_links = draw_corner_links(jax.random.fold_in(key_of[10], 71), 0)
    corner_codes = draw_corner_codes(jax.random.fold_in(key_of[10], 71), 0)
    gossip_bit = jax.random.randint(key_of[8], (1,), 0, 2).astype(jnp.int32)
    batch_size = jax.random.randint(key_of[9], (1,), 32, 513).astype(jnp.int32)
    return dict(fields=fields, cotangent=cotangent, weights=weights, ema=ema, tile_links=tile_links, tile_codes=tile_codes, corner_links=corner_links, corner_codes=corner_codes, gossip_bit=gossip_bit, batch_size=batch_size)


LEARN = 0.5

def edge_strips(block):
    return jnp.stack([block[:, 0], block[:, -1], block[:, :, 0], block[:, :, -1]], axis=1)

def corner_cells(block):
    return jnp.stack([block[:, 0, 0], block[:, 0, -1], block[:, -1, 0], block[:, -1, -1]], axis=1)

def padded_sides(block):
    return jnp.stack([block[:, 0, 1:-1], block[:, -1, 1:-1], block[:, 1:-1, 0], block[:, 1:-1, -1]], axis=1)

def with_halo(block, strips, corner_vals):
    top_row = jnp.concatenate([corner_vals[:, 0:1], strips[:, 0], corner_vals[:, 1:2]], axis=1)
    bottom_row = jnp.concatenate([corner_vals[:, 2:3], strips[:, 1], corner_vals[:, 3:4]], axis=1)
    middle = jnp.concatenate([strips[:, 2][:, :, None], block, strips[:, 3][:, :, None]], axis=2)
    return jnp.concatenate([top_row[:, None], middle, bottom_row[:, None]], axis=1)

def reference(fields, cotangent, weights, ema, tile_links, tile_codes, corner_links, corner_codes, gossip_bit, batch_size):
    present = (corner_links >= 0)[:, :, None]
    corner_source = jnp.maximum(corner_links, 0)
    weight_scale = (9.0 * C) ** (-0.5)

    def one_replica(packed):
        field_block, cot_block, weight_rows = packed
        kernel = (weight_rows * weight_scale).astype(jnp.bfloat16).reshape(C, 9, C)
        strips = edge_strips(field_block)[tile_links, tile_codes]
        corner_vals = jnp.where(present, corner_cells(field_block)[corner_source, corner_codes], jnp.zeros((), jnp.bfloat16))
        padded = with_halo(field_block, strips, corner_vals)
        hidden = jnp.zeros((TILES * TS * TS, C), jnp.float32)
        for tap_index in range(9):
            row_off, col_off = divmod(tap_index, 3)
            window = padded[:, row_off:row_off + TS, col_off:col_off + TS].reshape(-1, C)
            hidden = hidden + jnp.dot(window, kernel[:, tap_index, :], preferred_element_type=jnp.float32)
        sigmoid_pre = jax.nn.sigmoid(hidden)
        output = (hidden * sigmoid_pre).astype(jnp.bfloat16)
        grad_pre = (cot_block.reshape(-1, C).astype(jnp.float32) * (sigmoid_pre * (1.0 + hidden * (1.0 - sigmoid_pre)))).astype(jnp.bfloat16)
        pieces = []
        grad_pad = jnp.zeros((TILES, TS + 2, TS + 2, C), jnp.float32)
        for tap_index in range(9):
            row_off, col_off = divmod(tap_index, 3)
            window = padded[:, row_off:row_off + TS, col_off:col_off + TS].reshape(-1, C)
            pieces.append(jnp.dot(window.T, grad_pre, preferred_element_type=jnp.float32))
            backward = jnp.dot(grad_pre, kernel[:, tap_index, :].T, preferred_element_type=jnp.float32)
            grad_pad = grad_pad.at[:, row_off:row_off + TS, col_off:col_off + TS].add(backward.reshape(TILES, TS, TS, C))
        kernel_grad = jnp.stack(pieces, axis=1).reshape(9 * C, C)
        side_grad = lax.optimization_barrier(padded_sides(grad_pad).astype(jnp.bfloat16)).astype(jnp.float32)
        corner_grad = jnp.where(present, corner_cells(grad_pad), jnp.zeros((), jnp.float32))
        corner_grad = lax.optimization_barrier(corner_grad.astype(jnp.bfloat16)).astype(jnp.float32)
        returned = jnp.zeros((TILES, 4, TS, C), jnp.float32).at[tile_links, tile_codes].add(side_grad)
        corner_back = jnp.zeros((TILES, 4, C), jnp.float32).at[corner_source, corner_codes].add(corner_grad)
        interior = grad_pad[:, 1:-1, 1:-1]
        interior = interior.at[:, 0].add(returned[:, 0]).at[:, -1].add(returned[:, 1])
        interior = interior.at[:, :, 0].add(returned[:, 2]).at[:, :, -1].add(returned[:, 3])
        interior = interior.at[:, 0, 0].add(corner_back[:, 0]).at[:, 0, -1].add(corner_back[:, 1])
        interior = interior.at[:, -1, 0].add(corner_back[:, 2]).at[:, -1, -1].add(corner_back[:, 3])
        square_sum = jnp.sum(kernel_grad * kernel_grad)
        root_mean = jnp.sqrt(square_sum / (9.0 * C * C) + 1e-06)
        updated = weight_rows - LEARN * kernel_grad / root_mean
        return (output.reshape(TILES, TS, TS, C), interior.astype(jnp.bfloat16), updated)
    outputs, field_grads, updated = lax.map(one_replica, (fields, cotangent, weights))
    partner_ids = jnp.bitwise_xor(jnp.arange(REPS, dtype=jnp.int32), jnp.left_shift(jnp.int32(1), gossip_bit[0]))
    averaged = 0.5 * (updated + updated[partner_ids])
    decay = jnp.power(0.99, batch_size[0].astype(jnp.float32) / 32.0)
    ema_out = decay * ema + (1.0 - decay) * averaged
    return (outputs, field_grads, averaged, ema_out)
```

```python
import functools
import math

import jax
import jax.numpy as jnp
import numpy as np
from jax import lax
from jax.experimental import pallas as pl
from jax.experimental.pallas import tpu as pltpu
from jax.sharding import PartitionSpec as P

LEARN = 0.5
MESH = pl.DeviceIdType.MESH
VMEM = pl.BlockSpec(memory_space=pltpu.VMEM)
SMEM = pl.BlockSpec(memory_space=pltpu.SMEM)
LIMIT = 48 * 1024 * 1024
LANES = 128


def strip_lists(tiles, devices):
    sub = math.isqrt(tiles // 12)
    per = tiles // devices
    lists = [[] for _ in range(devices)]
    slot = np.full((tiles, 4), -1, np.int32)
    for tile in range(tiles):
        face, row, col = tile // (sub * sub), tile % (sub * sub) // sub, tile % sub
        owner = tile // per
        for edge, (down, right) in enumerate(((-1, 0), (1, 0), (0, -1), (0, 1))):
            r, c = row + down, col + right
            inside = 0 <= r < sub and 0 <= c < sub
            if inside and (face * sub * sub + r * sub + c) // per == owner:
                continue
            slot[tile, edge] = len(lists[owner])
            lists[owner].append((tile - owner * per) * 4 + edge)
    most = max(len(found) for found in lists)
    table = np.zeros((devices, most), np.int32)
    for owner, found in enumerate(lists):
        table[owner, : len(found)] = found
    return most, table, np.maximum(slot, 0)


def greet(peers):
    barrier = pltpu.get_barrier_semaphore()
    for peer in peers:
        pl.semaphore_signal(barrier, inc=1, device_id=peer, device_id_type=MESH)
    pl.semaphore_wait(barrier, len(peers))


def tile_peers(n):
    me = lax.axis_index("tile")
    return [{"tile": lax.rem(me + k, n)} for k in range(1, n)]


def send(src, dst, send_sem, recv_sem, peer):
    copy = pltpu.make_async_remote_copy(
        src_ref=src,
        dst_ref=dst,
        send_sem=send_sem,
        recv_sem=recv_sem,
        device_id=peer,
        device_id_type=MESH,
    )
    copy.start()
    return copy


def pack_strips(index, strips, corners, pack, count):
    @pl.loop(0, count)
    def _(k):
        pack[k] = strips[index[k]]

    pack[count:] = corners[...]


def gather_kernel(n, count, index, taps, strips, corners, all_taps, all_pack, pack, s1, r1, s2, r2):
    me = lax.axis_index("tile")
    peers = tile_peers(n)
    greet(peers)
    copies = []
    for k, peer in enumerate(peers):
        copies.append(send(taps, all_taps.at[me], s1.at[k], r1.at[k], peer))
    pack_strips(index, strips, corners, pack, count)
    for k, peer in enumerate(peers):
        copies.append(send(pack, all_pack.at[me], s2.at[k], r2.at[k], peer))
    all_taps[me] = taps[...]
    for copy in copies:
        copy.wait()


def put(ref, rows, value):
    for half in range(ref.shape[0]):
        ref[half, rows] = value[:, half * LANES : (half + 1) * LANES]


def get(ref, rows):
    return jnp.concatenate([ref[half, rows] for half in range(ref.shape[0])], axis=1)


def gain(ref, rows, value):
    for half in range(ref.shape[0]):
        ref[half, rows] = ref[half, rows] + value[:, half * LANES : (half + 1) * LANES]


def find_strip(refs, strips, all_pack, t, edge):
    me_ref, links, codes, _, _, slots = refs
    per = strips.shape[0] // 4
    at = t * 4 + edge
    link, code = links[at], codes[at]
    me = me_ref[0]
    owner = link // per
    here = jnp.clip((link - me * per) * 4 + code, 0, per * 4 - 1)
    own = strips[here].astype(jnp.float32)
    other = all_pack[owner, slots[link * 4 + code]].astype(jnp.float32)
    return jnp.where(owner == me, own, other)


def find_corner(refs, corners, all_pack, count, t, q):
    me_ref, _, _, corner_links, corner_codes, _ = refs
    per = corners.shape[0] * 2
    at = t * 4 + q
    link, code = corner_links[at], corner_codes[at]
    me = me_ref[0]
    safe = jnp.maximum(link, 0)
    owner = safe // per
    near = safe - owner * per
    own = corners[near // 2].astype(jnp.float32)
    other = all_pack[owner, count + near // 2].astype(jnp.float32)
    rows = jnp.where(owner == me, own, other)
    row = lax.rem(near, 2) * 4 + code
    chosen = lax.broadcasted_iota(jnp.int32, rows.shape, 0) == row
    chosen = chosen & (link >= 0)
    return jnp.sum(jnp.where(chosen, rows, 0.0), axis=0, keepdims=True)


def main_kernel(
    n, count, me_ref, links, codes, corner_links, corner_codes, slots,
    fields, cot, all_taps, all_pack, strips, corners,
    act, wgrad, inner, side_out, corner_out,
    e0, e1, e2, x0, x1, x2, kern, dpre, d0, d1, d2,
):
    refs = (me_ref, links, codes, corner_links, corner_codes, slots)
    side, wide = fields.shape[0], fields.shape[1]
    per = wide // side
    rc = all_taps.shape[2]
    f32 = jnp.float32
    for owner in range(n):
        for tap in range(9):
            kern[tap, owner * rc : (owner + 1) * rc] = all_taps[owner, tap]
    for i in range(side):
        put(e1, pl.ds((i + 1) * wide, wide), fields[i].astype(f32))

    @pl.loop(0, per)
    def _(t):
        at = pl.multiple_of(t * side, side)
        put(e1, pl.ds(at, side), find_strip(refs, strips, all_pack, t, 0))
        put(e1, pl.ds((side + 1) * wide + at, side), find_strip(refs, strips, all_pack, t, 1))

    for i in range(side + 2):
        rows = pl.ds(i * wide, wide)
        for half in range(e1.shape[0]):
            e0[half, rows] = pltpu.roll(e1[half, rows], 1, 0)
            e2[half, rows] = pltpu.roll(e1[half, rows], wide - 1, 0)

    @pl.loop(0, per)
    def _(t):
        at = t * side
        end = (side + 1) * wide + at
        put(e0, pl.ds(wide + at, side, stride=wide), find_strip(refs, strips, all_pack, t, 2))
        put(e2, pl.ds(wide + at + side - 1, side, stride=wide), find_strip(refs, strips, all_pack, t, 3))
        put(e0, pl.ds(at, 1), find_corner(refs, corners, all_pack, count, t, 0))
        put(e2, pl.ds(at + side - 1, 1), find_corner(refs, corners, all_pack, count, t, 1))
        put(e0, pl.ds(end, 1), find_corner(refs, corners, all_pack, count, t, 2))
        put(e2, pl.ds(end + side - 1, 1), find_corner(refs, corners, all_pack, count, t, 3))

    for x, e in ((x0, e0), (x1, e1), (x2, e2)):
        for half in range(e.shape[0]):
            x[:, half * LANES : (half + 1) * LANES] = e[half].astype(jnp.bfloat16)
    xs = (x0, x1, x2)

    dpre[0 : 2 * wide] = jnp.zeros((2 * wide, dpre.shape[1]), jnp.bfloat16)
    dpre[(side + 2) * wide :] = jnp.zeros((2 * wide, dpre.shape[1]), jnp.bfloat16)

    @pl.loop(0, side)
    def _(i):
        pre = None
        for tap in range(9):
            a, b = divmod(tap, 3)
            rows = xs[b][pl.ds(pl.multiple_of((i + a) * wide, 16), wide)]
            part = jnp.dot(rows, kern[tap], preferred_element_type=f32)
            pre = part if pre is None else pre + part
        s = jax.nn.sigmoid(pre)
        act[i] = (pre * s).astype(jnp.bfloat16)
        grad = cot[i].astype(f32) * (s * (1.0 + pre * (1.0 - s)))
        dpre[pl.ds(pl.multiple_of((i + 2) * wide, 16), wide)] = grad.astype(jnp.bfloat16)

    for tap in range(9):
        a, b = divmod(tap, 3)
        part = lax.dot_general(
            xs[b][a * wide : (a + side) * wide],
            dpre[2 * wide : (side + 2) * wide],
            (((0,), (0,)), ((), ())),
            preferred_element_type=f32,
        )
        for owner in range(n):
            wgrad[owner, tap] = part[owner * rc : (owner + 1) * rc].astype(jnp.bfloat16)

    @pl.loop(0, side + 2)
    def _(i):
        at = pl.multiple_of(i * wide, 16)
        found = []
        for b, d in enumerate((d0, d1, d2)):
            total = None
            for a in range(3):
                rows = dpre[pl.ds(pl.multiple_of((i - a + 2) * wide, 16), wide)]
                part = lax.dot_general(
                    rows, kern[3 * a + b], (((1,), (1,)), ((), ())), preferred_element_type=f32
                )
                total = part if total is None else total + part
            found.append(total)
        put(d0, pl.ds(at, wide), found[0])
        put(d2, pl.ds(at, wide), found[2])
        column = lax.rem(lax.broadcasted_iota(jnp.int32, found[0].shape, 0), side)
        left = jnp.where(column < side - 1, pltpu.roll(found[0], wide - 1, 0), 0.0)
        right = jnp.where(column > 0, pltpu.roll(found[2], 1, 0), 0.0)
        put(d1, pl.ds(at, wide), found[1] + left + right)

    inner[...] = d1[:, wide : (side + 1) * wide]
    last = (side + 1) * wide

    @pl.loop(0, per)
    def _(t):
        at = pl.multiple_of(t * side, side)
        side_out[t * 4] = get(d1, pl.ds(at, side)).astype(jnp.bfloat16)
        side_out[t * 4 + 1] = get(d1, pl.ds(last + at, side)).astype(jnp.bfloat16)
        side_out[t * 4 + 2] = get(d0, pl.ds(wide + at, side, stride=wide)).astype(jnp.bfloat16)
        side_out[t * 4 + 3] = get(d2, pl.ds(wide + at + side - 1, side, stride=wide)).astype(jnp.bfloat16)

    for pair in range(per // 2):
        rows = []
        for t in (2 * pair, 2 * pair + 1):
            at = t * side
            for d, row in ((d0, at), (d2, at + side - 1), (d0, last + at), (d2, last + at + side - 1)):
                rows.append(get(d, pl.ds(row, 1)))
        corner_out[pair] = jnp.concatenate(rows, axis=0).astype(jnp.bfloat16)


def reduce_kernel(
    n, count, levels, total_count, index, bit, wgrad, strips, corners, weights,
    averaged, all_pack,
    pack, slots, sums, updated, partner, s1, r1, s2, r2, s3, r3, s4, r4,
):
    me = lax.axis_index("tile")
    rep = lax.axis_index("rep")
    peers = tile_peers(n)
    friends = []
    for level in range(levels):
        step = 2**level
        friends.append({"rep": rep + step * (1 - 2 * lax.rem(rep // step, 2))})
    greet(peers + friends)
    copies = []
    for k, peer in enumerate(peers):
        copies.append(
            send(wgrad.at[lax.rem(me + k + 1, n)], slots.at[k], s1.at[k], r1.at[k], peer)
        )
    pack_strips(index, strips, corners, pack, count)
    packs = []
    for k, peer in enumerate(peers):
        packs.append(send(pack, all_pack.at[me], s2.at[k], r2.at[k], peer))
    grad = wgrad[me].astype(jnp.float32)
    for k, copy in enumerate(copies):
        copy.wait()
        grad = grad + slots[k].astype(jnp.float32)
    square = grad * grad
    lanes = sums.shape[2]
    square = jnp.sum(square.reshape(-1, 8, square.shape[2]), axis=0)
    sums[0] = sum(square[:, j : j + lanes] for j in range(0, square.shape[1], lanes))
    small = []
    for k, peer in enumerate(peers):
        small.append(send(sums.at[0], sums.at[k + 1], s3.at[k], r3.at[k], peer))
    for copy in small:
        copy.wait()
    mean = jnp.sum(sums[...], keepdims=True) / total_count
    updated[...] = weights[...] - LEARN * grad / jnp.sqrt(mean + 1e-06)
    swaps = []
    for level, friend in enumerate(friends):
        swaps.append(send(updated, partner.at[level], s4.at[level], r4.at[level], friend))
    for copy in swaps:
        copy.wait()
    averaged[...] = 0.5 * (updated[...] + partner[bit[0]])
    for copy in packs:
        copy.wait()


def finish_kernel(
    count, me_ref, links, codes, corner_links, corner_codes, slots,
    inner, all_pack, strips, corners, out, total,
):
    refs = (me_ref, links, codes, corner_links, corner_codes, slots)
    side, wide = out.shape[0], out.shape[1]
    per = wide // side
    total[...] = inner[...]
    last = (side - 1) * wide

    @pl.loop(0, per)
    def _(t):
        at = pl.multiple_of(t * side, side)
        first = pl.ds(at, side)
        gain(total, first, find_strip(refs, strips, all_pack, t, 0))
        end = pl.ds(last + at, side)
        gain(total, end, find_strip(refs, strips, all_pack, t, 1))
        left = pl.ds(at, side, stride=wide)
        gain(total, left, find_strip(refs, strips, all_pack, t, 2))
        right = pl.ds(at + side - 1, side, stride=wide)
        gain(total, right, find_strip(refs, strips, all_pack, t, 3))
        for q, row in enumerate((at, at + side - 1, last + at, last + at + side - 1)):
            cell = pl.ds(row, 1)
            gain(total, cell, find_corner(refs, corners, all_pack, count, t, q))

    for i in range(side):
        out[i] = get(total, pl.ds(i * wide, wide)).astype(jnp.bfloat16)


def body(
    fields, cotangent, weights, ema, tile_links, tile_codes, corner_links, corner_codes,
    gossip_bit, batch_size,
):
    block = fields[0]
    per, side, _, channels = block.shape
    n = lax.axis_size("tile")
    levels = lax.axis_size("rep").bit_length() - 1
    me = lax.axis_index("tile")
    count, table, slot_table = strip_lists(tile_links.shape[0], n)
    rows = weights.shape[1]
    rc = rows // 9
    bf16, f32 = jnp.bfloat16, jnp.float32
    total_count = 9.0 * channels * channels
    index = lax.dynamic_slice_in_dim(jnp.asarray(table), me, 1, 0)[0]
    blocks = count + per // 2

    def mine(array):
        return lax.dynamic_slice_in_dim(array, me * per, per, 0).reshape(-1)

    tables = (
        me.astype(jnp.int32).reshape(1),
        mine(tile_links),
        mine(tile_codes),
        mine(corner_links),
        mine(corner_codes),
        jnp.asarray(slot_table.reshape(-1)),
    )
    w_tap = weights[0].reshape(rc, 9, channels).transpose(1, 0, 2)
    taps = (w_tap * total_count_scale(channels)).astype(bf16)
    strips = jnp.stack([block[:, 0], block[:, -1], block[:, :, 0], block[:, :, -1]], axis=1)
    strips = strips.reshape(per * 4, side, channels)
    cells = jnp.stack(
        [block[:, 0, 0], block[:, 0, -1], block[:, -1, 0], block[:, -1, -1]], axis=1
    ).reshape(per // 2, 8, channels)

    params = functools.partial(pltpu.CompilerParams, vmem_limit_bytes=LIMIT)
    sems = [pltpu.SemaphoreType.DMA((n - 1,))] * 2
    pack_shape = pltpu.VMEM((blocks, side, channels), bf16)
    all_pack_shape = jax.ShapeDtypeStruct((n, blocks, side, channels), bf16)
    all_taps, all_pack = pl.pallas_call(
        functools.partial(gather_kernel, n, count),
        out_shape=(jax.ShapeDtypeStruct((n, 9, rc, channels), bf16), all_pack_shape),
        in_specs=[SMEM, VMEM, VMEM, VMEM],
        out_specs=(VMEM, VMEM),
        scratch_shapes=[pack_shape] + sems * 2,
        compiler_params=params(collective_id=0, has_side_effects=True),
    )(index, taps, strips, cells)

    wide = per * side

    def by_row(value):
        return value.transpose(1, 0, 2, 3).reshape(side, wide, channels)

    def by_tile(value):
        return value.reshape(side, per, side, channels).transpose(1, 0, 2, 3)[None]

    tall = (side + 2) * wide
    act, wgrad, inner, side_grads, corner_grads = pl.pallas_call(
        functools.partial(main_kernel, n, count),
        out_shape=(
            jax.ShapeDtypeStruct((side, wide, channels), bf16),
            jax.ShapeDtypeStruct((n, 9, rc, channels), bf16),
            jax.ShapeDtypeStruct((channels // LANES, side * wide, LANES), f32),
            jax.ShapeDtypeStruct((per * 4, side, channels), bf16),
            jax.ShapeDtypeStruct((per // 2, 8, channels), bf16),
        ),
        in_specs=[SMEM] * 6 + [VMEM] * 6,
        out_specs=(VMEM,) * 5,
        scratch_shapes=[pltpu.VMEM((channels // LANES, tall, LANES), f32)] * 3
        + [pltpu.VMEM((tall, channels), bf16)] * 3
        + [pltpu.VMEM((9, channels, channels), bf16)]
        + [pltpu.VMEM(((side + 4) * wide, channels), bf16)]
        + [pltpu.VMEM((channels // LANES, tall, LANES), f32)] * 3,
        compiler_params=params(),
    )(*tables, by_row(block), by_row(cotangent[0]), all_taps, all_pack, strips, cells)

    bit = jnp.clip(gossip_bit, 0, levels - 1)
    averaged, all_back = pl.pallas_call(
        functools.partial(reduce_kernel, n, count, levels, total_count),
        out_shape=(jax.ShapeDtypeStruct((9, rc, channels), f32), all_pack_shape),
        in_specs=[SMEM, SMEM, VMEM, VMEM, VMEM, VMEM],
        out_specs=(VMEM, VMEM),
        scratch_shapes=[
            pack_shape,
            pltpu.VMEM((n - 1, 9, rc, channels), bf16),
            pltpu.VMEM((n, 8, 128), f32),
            pltpu.VMEM((9, rc, channels), f32),
            pltpu.VMEM((levels, 9, rc, channels), f32),
        ]
        + sems * 3
        + [pltpu.SemaphoreType.DMA((levels,))] * 2,
        compiler_params=params(collective_id=1, has_side_effects=True),
    )(index, bit, wgrad, side_grads, corner_grads, w_tap)

    grads = pl.pallas_call(
        functools.partial(finish_kernel, count),
        out_shape=jax.ShapeDtypeStruct((side, wide, channels), bf16),
        in_specs=[SMEM] * 6 + [VMEM] * 4,
        out_specs=VMEM,
        scratch_shapes=[pltpu.VMEM((channels // LANES, side * wide, LANES), f32)],
        compiler_params=params(),
    )(*tables, inner, all_back, side_grads, corner_grads)

    averaged = averaged.transpose(1, 0, 2).reshape(rows, channels)
    decay = jnp.power(0.99, batch_size[0].astype(f32) / 32.0)
    ema_out = decay * ema[0] + (1.0 - decay) * averaged
    return by_tile(act), by_tile(grads), averaged[None], ema_out[None]


def total_count_scale(channels):
    return (9.0 * channels) ** (-0.5)


def solution(mesh):
    wide = P("rep", "tile", None, None, None)
    thin = P("rep", "tile", None)
    return jax.shard_map(
        body,
        mesh=mesh,
        in_specs=(wide, wide, thin, thin, P(), P(), P(), P(), P(), P()),
        out_specs=(wide, wide, thin, thin),
        check_vma=False,
    )
```

```python
import functools
import math

import jax
import jax.numpy as jnp
import numpy as np
from jax import lax
from jax.experimental import pallas as pl
from jax.experimental.pallas import tpu as pltpu
from jax.sharding import PartitionSpec as P

LEARN = 0.5
MESH = pl.DeviceIdType.MESH
VMEM = pl.BlockSpec(memory_space=pltpu.VMEM)
SMEM = pl.BlockSpec(memory_space=pltpu.SMEM)
LIMIT = 48 * 1024 * 1024
LANES = 128


def strip_lists(tiles, devices):
    sub = math.isqrt(tiles // 12)
    per = tiles // devices
    lists = [[] for _ in range(devices)]
    slot = np.full((tiles, 4), -1, np.int32)
    for tile in range(tiles):
        face, row, col = tile // (sub * sub), tile % (sub * sub) // sub, tile % sub
        owner = tile // per
        for edge, (down, right) in enumerate(((-1, 0), (1, 0), (0, -1), (0, 1))):
            r, c = row + down, col + right
            inside = 0 <= r < sub and 0 <= c < sub
            if inside and (face * sub * sub + r * sub + c) // per == owner:
                continue
            slot[tile, edge] = len(lists[owner])
            lists[owner].append((tile - owner * per) * 4 + edge)
    most = max(len(found) for found in lists)
    table = np.zeros((devices, most), np.int32)
    for owner, found in enumerate(lists):
        table[owner, : len(found)] = found
    return most, table, np.maximum(slot, 0)


def greet(peers):
    barrier = pltpu.get_barrier_semaphore()
    for peer in peers:
        pl.semaphore_signal(barrier, inc=1, device_id=peer, device_id_type=MESH)
    pl.semaphore_wait(barrier, len(peers))


def tile_peers(n):
    me = lax.axis_index("tile")
    return [{"tile": lax.rem(me + k, n)} for k in range(1, n)]


def send(src, dst, send_sem, recv_sem, peer):
    copy = pltpu.make_async_remote_copy(
        src_ref=src,
        dst_ref=dst,
        send_sem=send_sem,
        recv_sem=recv_sem,
        device_id=peer,
        device_id_type=MESH,
    )
    copy.start()
    return copy


def pack_strips(index, strips, corners, pack, count):
    @pl.loop(0, count)
    def _(k):
        pack[k] = strips[index[k]]

    pack[count:] = corners[...]


class Gather:
    def __init__(self, n, src, dst, sends, recvs):
        self.n, self.dst, self.sends, self.recvs = n, dst, sends, recvs
        me = lax.axis_index("tile")
        self.me = me
        self.mate = {"tile": me + 1 - 2 * lax.rem(me, 2)}
        self.first = []
        for k in range(1, n // 2):
            peer = {"tile": lax.rem(me + 2 * k, n)}
            self.first.append(send(src, dst.at[me], sends.at[k - 1], recvs.at[k - 1], peer))
        at = n // 2 - 1
        self.rest = [send(src, dst.at[me], sends.at[at], recvs.at[at], self.mate)]

    def forward(self):
        for k, copy in enumerate(self.first):
            copy.wait_recv()
            block = self.dst.at[lax.rem(self.me + self.n - 2 * (k + 1), self.n)]
            at = self.n // 2 + k
            self.rest.append(send(block, block, self.sends.at[at], self.recvs.at[at], self.mate))

    def finish(self):
        for copy in self.first:
            copy.wait_send()
        for copy in self.rest:
            copy.wait()


def gather_kernel(n, count, index, taps, strips, corners, all_taps, all_pack, pack, s1, r1, s2, r2):
    greet(tile_peers(n))
    one = Gather(n, taps, all_taps, s1, r1)
    pack_strips(index, strips, corners, pack, count)
    two = Gather(n, pack, all_pack, s2, r2)
    all_taps[lax.axis_index("tile")] = taps[...]
    one.forward()
    two.forward()
    one.finish()
    two.finish()


STEPS = 32000.0


def encode(value, code, scale):
    top = jnp.maximum(jnp.max(jnp.abs(value), axis=1, keepdims=True), 1e-30)
    code[...] = jnp.round(value * (STEPS / top)).astype(jnp.int32).astype(jnp.int16)
    scale[...] = top * (1.0 / STEPS)


def decode(code, scale):
    return code[...].astype(jnp.int32).astype(jnp.float32) * scale[...]


def put(ref, rows, value):
    for half in range(ref.shape[0]):
        ref[half, rows] = value[:, half * LANES : (half + 1) * LANES]


def get(ref, rows):
    return jnp.concatenate([ref[half, rows] for half in range(ref.shape[0])], axis=1)


def gain(ref, rows, value):
    for half in range(ref.shape[0]):
        ref[half, rows] = ref[half, rows] + value[:, half * LANES : (half + 1) * LANES]


def find_strip(refs, strips, all_pack, t, edge):
    me_ref, links, codes, _, _, slots = refs
    per = strips.shape[0] // 4
    at = t * 4 + edge
    link, code = links[at], codes[at]
    me = me_ref[0]
    owner = link // per
    here = jnp.clip((link - me * per) * 4 + code, 0, per * 4 - 1)
    own = strips[here].astype(jnp.float32)
    other = all_pack[owner, slots[link * 4 + code]].astype(jnp.float32)
    return jnp.where(owner == me, own, other)


def find_corner(refs, corners, all_pack, count, t, q):
    me_ref, _, _, corner_links, corner_codes, _ = refs
    per = corners.shape[0] * 2
    at = t * 4 + q
    link, code = corner_links[at], corner_codes[at]
    me = me_ref[0]
    safe = jnp.maximum(link, 0)
    owner = safe // per
    near = safe - owner * per
    own = corners[near // 2].astype(jnp.float32)
    other = all_pack[owner, count + near // 2].astype(jnp.float32)
    rows = jnp.where(owner == me, own, other)
    row = lax.rem(near, 2) * 4 + code
    chosen = lax.broadcasted_iota(jnp.int32, rows.shape, 0) == row
    chosen = chosen & (link >= 0)
    return jnp.sum(jnp.where(chosen, rows, 0.0), axis=0, keepdims=True)


def main_kernel(
    n, count, me_ref, links, codes, corner_links, corner_codes, slots,
    fields, cot, all_taps, all_pack, strips, corners,
    act, wgrad, inner, side_out, corner_out,
    e0, e1, e2, x0, x1, x2, kern, dpre, d0, d1, d2,
):
    refs = (me_ref, links, codes, corner_links, corner_codes, slots)
    side, wide = fields.shape[0], fields.shape[1]
    per = wide // side
    rc = all_taps.shape[2]
    f32 = jnp.float32
    for owner in range(n):
        for tap in range(9):
            kern[tap, owner * rc : (owner + 1) * rc] = all_taps[owner, tap]
    for i in range(side):
        put(e1, pl.ds((i + 1) * wide, wide), fields[i].astype(f32))

    @pl.loop(0, per)
    def _(t):
        at = pl.multiple_of(t * side, side)
        put(e1, pl.ds(at, side), find_strip(refs, strips, all_pack, t, 0))
        put(e1, pl.ds((side + 1) * wide + at, side), find_strip(refs, strips, all_pack, t, 1))

    for i in range(side + 2):
        rows = pl.ds(i * wide, wide)
        for half in range(e1.shape[0]):
            e0[half, rows] = pltpu.roll(e1[half, rows], 1, 0)
            e2[half, rows] = pltpu.roll(e1[half, rows], wide - 1, 0)

    @pl.loop(0, per)
    def _(t):
        at = t * side
        end = (side + 1) * wide + at
        put(e0, pl.ds(wide + at, side, stride=wide), find_strip(refs, strips, all_pack, t, 2))
        put(e2, pl.ds(wide + at + side - 1, side, stride=wide), find_strip(refs, strips, all_pack, t, 3))
        put(e0, pl.ds(at, 1), find_corner(refs, corners, all_pack, count, t, 0))
        put(e2, pl.ds(at + side - 1, 1), find_corner(refs, corners, all_pack, count, t, 1))
        put(e0, pl.ds(end, 1), find_corner(refs, corners, all_pack, count, t, 2))
        put(e2, pl.ds(end + side - 1, 1), find_corner(refs, corners, all_pack, count, t, 3))

    for x, e in ((x0, e0), (x1, e1), (x2, e2)):
        for half in range(e.shape[0]):
            x[:, half * LANES : (half + 1) * LANES] = e[half].astype(jnp.bfloat16)
    xs = (x0, x1, x2)

    dpre[0 : 2 * wide] = jnp.zeros((2 * wide, dpre.shape[1]), jnp.bfloat16)
    dpre[(side + 2) * wide :] = jnp.zeros((2 * wide, dpre.shape[1]), jnp.bfloat16)

    @pl.loop(0, side)
    def _(i):
        pre = None
        for tap in range(9):
            a, b = divmod(tap, 3)
            rows = xs[b][pl.ds(pl.multiple_of((i + a) * wide, 16), wide)]
            part = jnp.dot(rows, kern[tap], preferred_element_type=f32)
            pre = part if pre is None else pre + part
        s = jax.nn.sigmoid(pre)
        act[i] = (pre * s).astype(jnp.bfloat16)
        grad = cot[i].astype(f32) * (s * (1.0 + pre * (1.0 - s)))
        dpre[pl.ds(pl.multiple_of((i + 2) * wide, 16), wide)] = grad.astype(jnp.bfloat16)

    for tap in range(9):
        a, b = divmod(tap, 3)
        part = lax.dot_general(
            xs[b][a * wide : (a + side) * wide],
            dpre[2 * wide : (side + 2) * wide],
            (((0,), (0,)), ((), ())),
            preferred_element_type=f32,
        )
        for owner in range(n):
            wgrad[owner, tap] = part[owner * rc : (owner + 1) * rc]

    @pl.loop(0, side + 2)
    def _(i):
        at = pl.multiple_of(i * wide, 16)
        found = []
        for b, d in enumerate((d0, d1, d2)):
            total = None
            for a in range(3):
                rows = dpre[pl.ds(pl.multiple_of((i - a + 2) * wide, 16), wide)]
                part = lax.dot_general(
                    rows, kern[3 * a + b], (((1,), (1,)), ((), ())), preferred_element_type=f32
                )
                total = part if total is None else total + part
            found.append(total)
        put(d0, pl.ds(at, wide), found[0])
        put(d2, pl.ds(at, wide), found[2])
        column = lax.rem(lax.broadcasted_iota(jnp.int32, found[0].shape, 0), side)
        left = jnp.where(column < side - 1, pltpu.roll(found[0], wide - 1, 0), 0.0)
        right = jnp.where(column > 0, pltpu.roll(found[2], 1, 0), 0.0)
        put(d1, pl.ds(at, wide), found[1] + left + right)

    inner[...] = d1[:, wide : (side + 1) * wide]
    last = (side + 1) * wide

    @pl.loop(0, per)
    def _(t):
        at = pl.multiple_of(t * side, side)
        side_out[t * 4] = get(d1, pl.ds(at, side)).astype(jnp.bfloat16)
        side_out[t * 4 + 1] = get(d1, pl.ds(last + at, side)).astype(jnp.bfloat16)
        side_out[t * 4 + 2] = get(d0, pl.ds(wide + at, side, stride=wide)).astype(jnp.bfloat16)
        side_out[t * 4 + 3] = get(d2, pl.ds(wide + at + side - 1, side, stride=wide)).astype(jnp.bfloat16)

    for pair in range(per // 2):
        rows = []
        for t in (2 * pair, 2 * pair + 1):
            at = t * side
            for d, row in ((d0, at), (d2, at + side - 1), (d0, last + at), (d2, last + at + side - 1)):
                rows.append(get(d, pl.ds(row, 1)))
        corner_out[pair] = jnp.concatenate(rows, axis=0).astype(jnp.bfloat16)


def reduce_kernel(
    n, count, levels, total_count, index, bit, wgrad, strips, corners, weights,
    averaged, all_pack,
    pack, out_y, out_ys, in_y, in_ys, out_z, out_zs, in_z, in_zs, sums, updated, partner,
    s1, r1, s2, r2, s3, r3, s4, r4, s5, r5, s6, r6, s7, r7,
):
    me = lax.axis_index("tile")
    rep = lax.axis_index("rep")
    peers = tile_peers(n)
    friends = []
    for level in range(levels):
        step = 2**level
        friends.append({"rep": rep + step * (1 - 2 * lax.rem(rep // step, 2))})
    greet(peers + friends)
    line = n // 2
    odd = lax.rem(me, 2)
    mate = {"tile": me + 1 - 2 * odd}
    order = list(range(1, line)) + [0]
    near, far = {}, {}
    for k in order:
        there = lax.rem(me - odd + 2 * k, n) + 1 - odd
        encode(wgrad[there], out_y.at[k], out_ys.at[k])
        near[k] = (
            send(out_y.at[k], in_y.at[k], s1.at[k], r1.at[k], mate),
            send(out_ys.at[k], in_ys.at[k], s2.at[k], r2.at[k], mate),
        )
    pack_strips(index, strips, corners, pack, count)
    halo = Gather(n, pack, all_pack, s7, r7)
    grad = None
    for k in order:
        for copy in near[k]:
            copy.wait()
        there = lax.rem(me + 2 * k, n)
        grad = wgrad[there] + decode(in_y.at[k], in_ys.at[k])
        if k > 0:
            encode(grad, out_z.at[k - 1], out_zs.at[k - 1])
            peer = {"tile": there}
            far[k] = (
                send(out_z.at[k - 1], in_z.at[k - 1], s3.at[k - 1], r3.at[k - 1], peer),
                send(out_zs.at[k - 1], in_zs.at[k - 1], s4.at[k - 1], r4.at[k - 1], peer),
            )
    halo.forward()
    for k in far:
        for copy in far[k]:
            copy.wait()
        grad = grad + decode(in_z.at[k - 1], in_zs.at[k - 1])
    square = grad * grad
    lanes = sums.shape[2]
    square = jnp.sum(square.reshape(-1, 8, square.shape[2]), axis=0)
    sums[0] = sum(square[:, j : j + lanes] for j in range(0, square.shape[1], lanes))
    small = []
    for k, peer in enumerate(peers):
        small.append(send(sums.at[0], sums.at[k + 1], s5.at[k], r5.at[k], peer))
    for copy in small:
        copy.wait()
    mean = jnp.sum(sums[...], keepdims=True) / total_count
    updated[...] = weights[...] - LEARN * grad / jnp.sqrt(mean + 1e-06)
    swaps = []
    for level, friend in enumerate(friends):
        swaps.append(send(updated, partner.at[level], s6.at[level], r6.at[level], friend))
    for copy in swaps:
        copy.wait()
    averaged[...] = 0.5 * (updated[...] + partner[bit[0]])
    halo.finish()


def finish_kernel(
    count, me_ref, links, codes, corner_links, corner_codes, slots,
    inner, all_pack, strips, corners, out, total,
):
    refs = (me_ref, links, codes, corner_links, corner_codes, slots)
    side, wide = out.shape[0], out.shape[1]
    per = wide // side
    total[...] = inner[...]
    last = (side - 1) * wide

    @pl.loop(0, per)
    def _(t):
        at = pl.multiple_of(t * side, side)
        first = pl.ds(at, side)
        gain(total, first, find_strip(refs, strips, all_pack, t, 0))
        end = pl.ds(last + at, side)
        gain(total, end, find_strip(refs, strips, all_pack, t, 1))
        left = pl.ds(at, side, stride=wide)
        gain(total, left, find_strip(refs, strips, all_pack, t, 2))
        right = pl.ds(at + side - 1, side, stride=wide)
        gain(total, right, find_strip(refs, strips, all_pack, t, 3))
        for q, row in enumerate((at, at + side - 1, last + at, last + at + side - 1)):
            cell = pl.ds(row, 1)
            gain(total, cell, find_corner(refs, corners, all_pack, count, t, q))

    for i in range(side):
        out[i] = get(total, pl.ds(i * wide, wide)).astype(jnp.bfloat16)


def body(
    fields, cotangent, weights, ema, tile_links, tile_codes, corner_links, corner_codes,
    gossip_bit, batch_size,
):
    block = fields[0]
    per, side, _, channels = block.shape
    n = lax.axis_size("tile")
    line = n // 2
    levels = lax.axis_size("rep").bit_length() - 1
    me = lax.axis_index("tile")
    count, table, slot_table = strip_lists(tile_links.shape[0], n)
    rows = weights.shape[1]
    rc = rows // 9
    bf16, f32 = jnp.bfloat16, jnp.float32
    total_count = 9.0 * channels * channels
    index = lax.dynamic_slice_in_dim(jnp.asarray(table), me, 1, 0)[0]
    blocks = count + per // 2

    def mine(array):
        return lax.dynamic_slice_in_dim(array, me * per, per, 0).reshape(-1)

    tables = (
        me.astype(jnp.int32).reshape(1),
        mine(tile_links),
        mine(tile_codes),
        mine(corner_links),
        mine(corner_codes),
        jnp.asarray(slot_table.reshape(-1)),
    )
    w_tap = weights[0].reshape(rc, 9, channels).transpose(1, 0, 2)
    taps = (w_tap * total_count_scale(channels)).astype(bf16)
    strips = jnp.stack([block[:, 0], block[:, -1], block[:, :, 0], block[:, :, -1]], axis=1)
    strips = strips.reshape(per * 4, side, channels)
    cells = jnp.stack(
        [block[:, 0, 0], block[:, 0, -1], block[:, -1, 0], block[:, -1, -1]], axis=1
    ).reshape(per // 2, 8, channels)

    params = functools.partial(pltpu.CompilerParams, vmem_limit_bytes=LIMIT)
    sems = [pltpu.SemaphoreType.DMA((n - 1,))] * 2
    pack_shape = pltpu.VMEM((blocks, side, channels), bf16)
    all_pack_shape = jax.ShapeDtypeStruct((n, blocks, side, channels), bf16)
    all_taps, all_pack = pl.pallas_call(
        functools.partial(gather_kernel, n, count),
        out_shape=(jax.ShapeDtypeStruct((n, 9, rc, channels), bf16), all_pack_shape),
        in_specs=[SMEM, VMEM, VMEM, VMEM],
        out_specs=(VMEM, VMEM),
        scratch_shapes=[pack_shape] + sems * 2,
        compiler_params=params(collective_id=0, has_side_effects=True),
    )(index, taps, strips, cells)

    wide = per * side

    def by_row(value):
        return value.transpose(1, 0, 2, 3).reshape(side, wide, channels)

    def by_tile(value):
        return value.reshape(side, per, side, channels).transpose(1, 0, 2, 3)[None]

    tall = (side + 2) * wide
    act, wgrad, inner, side_grads, corner_grads = pl.pallas_call(
        functools.partial(main_kernel, n, count),
        out_shape=(
            jax.ShapeDtypeStruct((side, wide, channels), bf16),
            jax.ShapeDtypeStruct((n, 9, rc, channels), f32),
            jax.ShapeDtypeStruct((channels // LANES, side * wide, LANES), f32),
            jax.ShapeDtypeStruct((per * 4, side, channels), bf16),
            jax.ShapeDtypeStruct((per // 2, 8, channels), bf16),
        ),
        in_specs=[SMEM] * 6 + [VMEM] * 6,
        out_specs=(VMEM,) * 5,
        scratch_shapes=[pltpu.VMEM((channels // LANES, tall, LANES), f32)] * 3
        + [pltpu.VMEM((tall, channels), bf16)] * 3
        + [pltpu.VMEM((9, channels, channels), bf16)]
        + [pltpu.VMEM(((side + 4) * wide, channels), bf16)]
        + [pltpu.VMEM((channels // LANES, tall, LANES), f32)] * 3,
        compiler_params=params(),
    )(*tables, by_row(block), by_row(cotangent[0]), all_taps, all_pack, strips, cells)

    bit = jnp.clip(gossip_bit, 0, levels - 1)
    averaged, all_back = pl.pallas_call(
        functools.partial(reduce_kernel, n, count, levels, total_count),
        out_shape=(jax.ShapeDtypeStruct((9, rc, channels), f32), all_pack_shape),
        in_specs=[SMEM, SMEM, VMEM, VMEM, VMEM, VMEM],
        out_specs=(VMEM, VMEM),
        scratch_shapes=[
            pack_shape,
            pltpu.VMEM((line, 9, rc, channels), jnp.int16),
            pltpu.VMEM((line, 9, 1, channels), f32),
            pltpu.VMEM((line, 9, rc, channels), jnp.int16),
            pltpu.VMEM((line, 9, 1, channels), f32),
            pltpu.VMEM((line - 1, 9, rc, channels), jnp.int16),
            pltpu.VMEM((line - 1, 9, 1, channels), f32),
            pltpu.VMEM((line - 1, 9, rc, channels), jnp.int16),
            pltpu.VMEM((line - 1, 9, 1, channels), f32),
            pltpu.VMEM((n, 8, 128), f32),
            pltpu.VMEM((9, rc, channels), f32),
            pltpu.VMEM((levels, 9, rc, channels), f32),
        ]
        + [pltpu.SemaphoreType.DMA((line,))] * 4
        + [pltpu.SemaphoreType.DMA((line - 1,))] * 4
        + sems
        + [pltpu.SemaphoreType.DMA((levels,))] * 2
        + sems,
        compiler_params=params(collective_id=1, has_side_effects=True),
    )(index, bit, wgrad, side_grads, corner_grads, w_tap)

    grads = pl.pallas_call(
        functools.partial(finish_kernel, count),
        out_shape=jax.ShapeDtypeStruct((side, wide, channels), bf16),
        in_specs=[SMEM] * 6 + [VMEM] * 4,
        out_specs=VMEM,
        scratch_shapes=[pltpu.VMEM((channels // LANES, side * wide, LANES), f32)],
        compiler_params=params(),
    )(*tables, inner, all_back, side_grads, corner_grads)

    averaged = averaged.transpose(1, 0, 2).reshape(rows, channels)
    decay = jnp.power(0.99, batch_size[0].astype(f32) / 32.0)
    ema_out = decay * ema[0] + (1.0 - decay) * averaged
    return by_tile(act), by_tile(grads), averaged[None], ema_out[None]


def total_count_scale(channels):
    return (9.0 * channels) ** (-0.5)


def solution(mesh):
    wide = P("rep", "tile", None, None, None)
    thin = P("rep", "tile", None)
    return jax.shard_map(
        body,
        mesh=mesh,
        in_specs=(wide, wide, thin, thin, P(), P(), P(), P(), P(), P()),
        out_specs=(wide, wide, thin, thin),
        check_vma=False,
    )
```

```python
import functools
import math

import jax
import jax.numpy as jnp
import numpy as np
from jax import lax
from jax.experimental import pallas as pl
from jax.experimental.pallas import tpu as pltpu
from jax.sharding import PartitionSpec as P

LEARN = 0.5
MESH = pl.DeviceIdType.MESH
VMEM = pl.BlockSpec(memory_space=pltpu.VMEM)
SMEM = pl.BlockSpec(memory_space=pltpu.SMEM)
LIMIT = 48 * 1024 * 1024
LANES = 128


def strip_lists(tiles, devices, side):
    sub = math.isqrt(tiles // 12)
    per = tiles // devices
    lists = [[] for _ in range(devices)]
    slot = np.full((tiles, 4), -1, np.int32)
    end_slot = np.zeros((tiles, 4), np.int32)
    end_row = np.zeros((tiles, 4), np.int32)

    def split(tile):
        return tile // (sub * sub), tile % (sub * sub) // sub, tile % sub

    def near(tile, down, right):
        face, row, col = split(tile)
        r, c = row + down, col + right
        inside = 0 <= r < sub and 0 <= c < sub
        return inside and (face * sub * sub + r * sub + c) // per == tile // per

    def add(tile, edge):
        found = lists[tile // per]
        slot[tile, edge] = len(found)
        found.append(tile % per * 4 + edge)

    for tile in range(tiles):
        for edge, (down, right) in enumerate(((-1, 0), (1, 0), (0, -1), (0, 1))):
            if not near(tile, down, right):
                add(tile, edge)
    for tile in range(tiles):
        for q in range(4):
            a, b = divmod(q, 2)
            if near(tile, 2 * a - 1, 2 * b - 1):
                continue
            if slot[tile, a] < 0 and slot[tile, 2 + b] < 0:
                add(tile, a)
            if slot[tile, a] >= 0:
                end_slot[tile, q], end_row[tile, q] = slot[tile, a], b * (side - 1)
            else:
                end_slot[tile, q], end_row[tile, q] = slot[tile, 2 + b], a * (side - 1)
    most = max(len(found) for found in lists)
    table = np.zeros((devices, most), np.int32)
    for owner, found in enumerate(lists):
        table[owner, : len(found)] = found
    return most, table, np.maximum(slot, 0), end_slot, end_row


def greet(peers):
    barrier = pltpu.get_barrier_semaphore()
    for peer in peers:
        pl.semaphore_signal(barrier, inc=1, device_id=peer, device_id_type=MESH)
    pl.semaphore_wait(barrier, len(peers))


def tile_peers(n):
    me = lax.axis_index("tile")
    return [{"tile": lax.rem(me + k, n)} for k in range(1, n)]


def send(src, dst, send_sem, recv_sem, peer):
    copy = pltpu.make_async_remote_copy(
        src_ref=src,
        dst_ref=dst,
        send_sem=send_sem,
        recv_sem=recv_sem,
        device_id=peer,
        device_id_type=MESH,
    )
    copy.start()
    return copy


def pack_strips(index, strips, corners, pack, count):
    @pl.loop(0, count)
    def _(k):
        pack[k] = strips[index[k]]

    pack[count:] = corners[...]


class Gather:
    def __init__(self, n, src, dst, rows, sends, recvs):
        self.n, self.dst, self.rows, self.sends, self.recvs = n, dst, rows, sends, recvs
        me = lax.axis_index("tile")
        self.me = me
        self.mate = {"tile": me + 1 - 2 * lax.rem(me, 2)}
        self.first = []
        for k in range(1, n // 2):
            peer = {"tile": lax.rem(me + 2 * k, n)}
            self.first.append(send(src, dst.at[me, rows], sends.at[k - 1], recvs.at[k - 1], peer))
        at = n // 2 - 1
        self.rest = [send(src, dst.at[me, rows], sends.at[at], recvs.at[at], self.mate)]

    def forward(self):
        for k, copy in enumerate(self.first):
            copy.wait_recv()
            block = self.dst.at[lax.rem(self.me + self.n - 2 * (k + 1), self.n), self.rows]
            at = self.n // 2 + k
            self.rest.append(send(block, block, self.sends.at[at], self.recvs.at[at], self.mate))

    def finish(self):
        for copy in self.first:
            copy.wait_send()
        for copy in self.rest:
            copy.wait()


def gather_kernel(n, count, index, taps, strips, all_taps, all_pack, pack, *sems):
    greet(tile_peers(n))
    me = lax.axis_index("tile")
    parts = []
    for c in range(3):
        rows = pl.ds(3 * c, 3)
        parts.append(Gather(n, taps.at[rows], all_taps, rows, *sems[2 * c : 2 * c + 2]))

    @pl.loop(0, count)
    def _(k):
        pack[k] = strips[index[k]]

    cut = count // 2
    for c, rows in enumerate((pl.ds(0, cut), pl.ds(cut, count - cut))):
        parts.append(Gather(n, pack.at[rows], all_pack, rows, *sems[2 * c + 6 : 2 * c + 8]))
    all_taps[me] = taps[...]
    for part in parts:
        part.forward()
    for part in parts:
        part.finish()


STEPS = 32000.0


def encode(value, code, scale):
    top = jnp.maximum(jnp.max(jnp.abs(value), axis=1, keepdims=True), 1e-30)
    code[...] = jnp.round(value * (STEPS / top)).astype(jnp.int32).astype(jnp.int16)
    scale[...] = top * (1.0 / STEPS)


def decode(code, scale):
    return code[...].astype(jnp.int32).astype(jnp.float32) * scale[...]


def put(ref, rows, value):
    for half in range(ref.shape[0]):
        ref[half, rows] = value[:, half * LANES : (half + 1) * LANES]


def get(ref, rows):
    return jnp.concatenate([ref[half, rows] for half in range(ref.shape[0])], axis=1)


def gain(ref, rows, value):
    for half in range(ref.shape[0]):
        ref[half, rows] = ref[half, rows] + value[:, half * LANES : (half + 1) * LANES]


def find_strip(refs, strips, all_pack, t, edge):
    me_ref, links, codes, _, _, slots = refs
    per = strips.shape[0] // 4
    at = t * 4 + edge
    link, code = links[at], codes[at]
    me = me_ref[0]
    owner = link // per
    here = jnp.clip((link - me * per) * 4 + code, 0, per * 4 - 1)
    own = strips[here].astype(jnp.float32)
    other = all_pack[owner, slots[link * 4 + code]].astype(jnp.float32)
    return jnp.where(owner == me, own, other)


def find_end(refs, ends, strips, all_pack, t, q):
    me_ref, _, _, corner_links, corner_codes, _ = refs
    end_slot, end_row = ends
    per, side = strips.shape[0] // 4, strips.shape[1]
    at = t * 4 + q
    link, code = corner_links[at], corner_codes[at]
    me = me_ref[0]
    safe = jnp.maximum(link, 0)
    owner = safe // per
    own = strips[(safe - owner * per) * 4 + code // 2].astype(jnp.float32)
    other = all_pack[owner, end_slot[safe * 4 + code]].astype(jnp.float32)
    rows = jnp.where(owner == me, own, other)
    row = jnp.where(owner == me, lax.rem(code, 2) * (side - 1), end_row[safe * 4 + code])
    chosen = lax.broadcasted_iota(jnp.int32, rows.shape, 0) == row
    chosen = chosen & (link >= 0)
    return jnp.sum(jnp.where(chosen, rows, 0.0), axis=0, keepdims=True)


def find_corner(refs, corners, all_pack, count, t, q):
    me_ref, _, _, corner_links, corner_codes, _ = refs
    per = corners.shape[0] * 2
    at = t * 4 + q
    link, code = corner_links[at], corner_codes[at]
    me = me_ref[0]
    safe = jnp.maximum(link, 0)
    owner = safe // per
    near = safe - owner * per
    own = corners[near // 2].astype(jnp.float32)
    other = all_pack[owner, count + near // 2].astype(jnp.float32)
    rows = jnp.where(owner == me, own, other)
    row = lax.rem(near, 2) * 4 + code
    chosen = lax.broadcasted_iota(jnp.int32, rows.shape, 0) == row
    chosen = chosen & (link >= 0)
    return jnp.sum(jnp.where(chosen, rows, 0.0), axis=0, keepdims=True)


def main_kernel(
    n, me_ref, links, codes, corner_links, corner_codes, slots, end_slot, end_row,
    fields, cot, all_taps, all_pack, strips,
    act, wgrad, kern, dpre,
    e0, e1, e2, x0, x1, x2,
):
    refs = (me_ref, links, codes, corner_links, corner_codes, slots)
    ends = (end_slot, end_row)
    side, wide = fields.shape[0], fields.shape[1]
    per = wide // side
    rc = all_taps.shape[2]
    f32 = jnp.float32
    for owner in range(n):
        for tap in range(9):
            kern[tap, owner * rc : (owner + 1) * rc] = all_taps[owner, tap]
    for i in range(side):
        put(e1, pl.ds((i + 1) * wide, wide), fields[i].astype(f32))

    @pl.loop(0, per)
    def _(t):
        at = pl.multiple_of(t * side, side)
        put(e1, pl.ds(at, side), find_strip(refs, strips, all_pack, t, 0))
        put(e1, pl.ds((side + 1) * wide + at, side), find_strip(refs, strips, all_pack, t, 1))

    for i in range(side + 2):
        rows = pl.ds(i * wide, wide)
        for half in range(e1.shape[0]):
            e0[half, rows] = pltpu.roll(e1[half, rows], 1, 0)
            e2[half, rows] = pltpu.roll(e1[half, rows], wide - 1, 0)

    @pl.loop(0, per)
    def _(t):
        at = t * side
        end = (side + 1) * wide + at
        put(e0, pl.ds(wide + at, side, stride=wide), find_strip(refs, strips, all_pack, t, 2))
        put(e2, pl.ds(wide + at + side - 1, side, stride=wide), find_strip(refs, strips, all_pack, t, 3))
        put(e0, pl.ds(at, 1), find_end(refs, ends, strips, all_pack, t, 0))
        put(e2, pl.ds(at + side - 1, 1), find_end(refs, ends, strips, all_pack, t, 1))
        put(e0, pl.ds(end, 1), find_end(refs, ends, strips, all_pack, t, 2))
        put(e2, pl.ds(end + side - 1, 1), find_end(refs, ends, strips, all_pack, t, 3))

    for x, e in ((x0, e0), (x1, e1), (x2, e2)):
        for half in range(e.shape[0]):
            x[:, half * LANES : (half + 1) * LANES] = e[half].astype(jnp.bfloat16)
    xs = (x0, x1, x2)

    dpre[0 : 2 * wide] = jnp.zeros((2 * wide, dpre.shape[1]), jnp.bfloat16)
    dpre[(side + 2) * wide :] = jnp.zeros((2 * wide, dpre.shape[1]), jnp.bfloat16)

    @pl.loop(0, side)
    def _(i):
        pre = None
        for tap in range(9):
            a, b = divmod(tap, 3)
            rows = xs[b][pl.ds(pl.multiple_of((i + a) * wide, 16), wide)]
            part = jnp.dot(rows, kern[tap], preferred_element_type=f32)
            pre = part if pre is None else pre + part
        s = jax.nn.sigmoid(pre)
        act[i] = (pre * s).astype(jnp.bfloat16)
        grad = cot[i].astype(f32) * (s * (1.0 + pre * (1.0 - s)))
        dpre[pl.ds(pl.multiple_of((i + 2) * wide, 16), wide)] = grad.astype(jnp.bfloat16)

    for tap in range(9):
        a, b = divmod(tap, 3)
        part = lax.dot_general(
            xs[b][a * wide : (a + side) * wide],
            dpre[2 * wide : (side + 2) * wide],
            (((0,), (0,)), ((), ())),
            preferred_element_type=f32,
        )
        for owner in range(n):
            wgrad[owner, tap] = part[owner * rc : (owner + 1) * rc]


def back_field(kern, dpre, inner, side_out, corner_out, d0, d1, d2):
    f32 = jnp.float32
    per, side = side_out.shape[0] // 4, side_out.shape[1]
    wide = per * side

    @pl.loop(0, side + 2)
    def _(i):
        at = pl.multiple_of(i * wide, 16)
        found = []
        for b, d in enumerate((d0, d1, d2)):
            total = None
            for a in range(3):
                rows = dpre[pl.ds(pl.multiple_of((i - a + 2) * wide, 16), wide)]
                part = lax.dot_general(
                    rows, kern[3 * a + b], (((1,), (1,)), ((), ())), preferred_element_type=f32
                )
                total = part if total is None else total + part
            found.append(total)
        put(d0, pl.ds(at, wide), found[0])
        put(d2, pl.ds(at, wide), found[2])
        column = lax.rem(lax.broadcasted_iota(jnp.int32, found[0].shape, 0), side)
        left = jnp.where(column < side - 1, pltpu.roll(found[0], wide - 1, 0), 0.0)
        right = jnp.where(column > 0, pltpu.roll(found[2], 1, 0), 0.0)
        put(d1, pl.ds(at, wide), found[1] + left + right)

    inner[...] = d1[:, wide : (side + 1) * wide]
    last = (side + 1) * wide

    @pl.loop(0, per)
    def _(t):
        at = pl.multiple_of(t * side, side)
        side_out[t * 4] = get(d1, pl.ds(at, side)).astype(jnp.bfloat16)
        side_out[t * 4 + 1] = get(d1, pl.ds(last + at, side)).astype(jnp.bfloat16)
        side_out[t * 4 + 2] = get(d0, pl.ds(wide + at, side, stride=wide)).astype(jnp.bfloat16)
        side_out[t * 4 + 3] = get(d2, pl.ds(wide + at + side - 1, side, stride=wide)).astype(jnp.bfloat16)

    for pair in range(per // 2):
        rows = []
        for t in (2 * pair, 2 * pair + 1):
            at = t * side
            for d, row in ((d0, at), (d2, at + side - 1), (d0, last + at), (d2, last + at + side - 1)):
                rows.append(get(d, pl.ds(row, 1)))
        corner_out[pair] = jnp.concatenate(rows, axis=0).astype(jnp.bfloat16)


def reduce_kernel(
    n, count, levels, total_count, index, bit, wgrad, kern, dpre, weights,
    averaged, all_pack, inner, strips, corners,
    d0, d1, d2, pack, out_y, out_ys, in_y, in_ys, out_z, out_zs, in_z, in_zs, sums, updated, partner,
    s1, r1, s2, r2, s3, r3, s4, r4, s5, r5, s6, r6, s7, r7,
):
    me = lax.axis_index("tile")
    rep = lax.axis_index("rep")
    peers = tile_peers(n)
    friends = []
    for level in range(levels):
        step = 2**level
        friends.append({"rep": rep + step * (1 - 2 * lax.rem(rep // step, 2))})
    greet(peers + friends)
    line = n // 2
    odd = lax.rem(me, 2)
    mate = {"tile": me + 1 - 2 * odd}
    order = list(range(1, line)) + [0]
    near, far = {}, {}
    for k in order:
        there = lax.rem(me - odd + 2 * k, n) + 1 - odd
        encode(wgrad[there], out_y.at[k], out_ys.at[k])
        near[k] = (
            send(out_y.at[k], in_y.at[k], s1.at[k], r1.at[k], mate),
            send(out_ys.at[k], in_ys.at[k], s2.at[k], r2.at[k], mate),
        )
    back_field(kern, dpre, inner, strips, corners, d0, d1, d2)
    pack_strips(index, strips, corners, pack, count)
    cut = pack.shape[0] // 2
    halo = []
    for c, rows in enumerate((pl.ds(0, cut), pl.ds(cut, pack.shape[0] - cut))):
        halo.append(Gather(n, pack.at[rows], all_pack, rows, s7.at[c], r7.at[c]))
    grad = None
    for k in order:
        for copy in near[k]:
            copy.wait()
        there = lax.rem(me + 2 * k, n)
        grad = wgrad[there] + decode(in_y.at[k], in_ys.at[k])
        if k > 0:
            encode(grad, out_z.at[k - 1], out_zs.at[k - 1])
            peer = {"tile": there}
            far[k] = (
                send(out_z.at[k - 1], in_z.at[k - 1], s3.at[k - 1], r3.at[k - 1], peer),
                send(out_zs.at[k - 1], in_zs.at[k - 1], s4.at[k - 1], r4.at[k - 1], peer),
            )
    for part in halo:
        part.forward()
    for k in far:
        for copy in far[k]:
            copy.wait()
        grad = grad + decode(in_z.at[k - 1], in_zs.at[k - 1])
    square = grad * grad
    lanes = sums.shape[2]
    square = jnp.sum(square.reshape(-1, 8, square.shape[2]), axis=0)
    sums[0] = sum(square[:, j : j + lanes] for j in range(0, square.shape[1], lanes))
    small = []
    for k, peer in enumerate(peers):
        small.append(send(sums.at[0], sums.at[k + 1], s5.at[k], r5.at[k], peer))
    for copy in small:
        copy.wait()
    mean = jnp.sum(sums[...], keepdims=True) / total_count
    updated[...] = weights[...] - LEARN * grad / jnp.sqrt(mean + 1e-06)
    swaps = []
    for level, friend in enumerate(friends):
        swaps.append(send(updated, partner.at[level], s6.at[level], r6.at[level], friend))
    for copy in swaps:
        copy.wait()
    averaged[...] = 0.5 * (updated[...] + partner[bit[0]])
    for part in halo:
        part.finish()


def finish_kernel(
    count, me_ref, links, codes, corner_links, corner_codes, slots,
    inner, all_pack, strips, corners, out, total,
):
    refs = (me_ref, links, codes, corner_links, corner_codes, slots)
    side, wide = out.shape[0], out.shape[1]
    per = wide // side
    total[...] = inner[...]
    last = (side - 1) * wide

    @pl.loop(0, per)
    def _(t):
        at = pl.multiple_of(t * side, side)
        first = pl.ds(at, side)
        gain(total, first, find_strip(refs, strips, all_pack, t, 0))
        end = pl.ds(last + at, side)
        gain(total, end, find_strip(refs, strips, all_pack, t, 1))
        left = pl.ds(at, side, stride=wide)
        gain(total, left, find_strip(refs, strips, all_pack, t, 2))
        right = pl.ds(at + side - 1, side, stride=wide)
        gain(total, right, find_strip(refs, strips, all_pack, t, 3))
        for q, row in enumerate((at, at + side - 1, last + at, last + at + side - 1)):
            cell = pl.ds(row, 1)
            gain(total, cell, find_corner(refs, corners, all_pack, count, t, q))

    for i in range(side):
        out[i] = get(total, pl.ds(i * wide, wide)).astype(jnp.bfloat16)


def body(
    fields, cotangent, weights, ema, tile_links, tile_codes, corner_links, corner_codes,
    gossip_bit, batch_size,
):
    block = fields[0]
    per, side, _, channels = block.shape
    n = lax.axis_size("tile")
    line = n // 2
    levels = lax.axis_size("rep").bit_length() - 1
    me = lax.axis_index("tile")
    count, table, slot_table, end_slot, end_row = strip_lists(tile_links.shape[0], n, side)
    rows = weights.shape[1]
    rc = rows // 9
    bf16, f32 = jnp.bfloat16, jnp.float32
    total_count = 9.0 * channels * channels
    index = lax.dynamic_slice_in_dim(jnp.asarray(table), me, 1, 0)[0]
    blocks = count + per // 2

    def mine(array):
        return lax.dynamic_slice_in_dim(array, me * per, per, 0).reshape(-1)

    tables = (
        me.astype(jnp.int32).reshape(1),
        mine(tile_links),
        mine(tile_codes),
        mine(corner_links),
        mine(corner_codes),
        jnp.asarray(slot_table.reshape(-1)),
    )
    w_tap = weights[0].reshape(rc, 9, channels).transpose(1, 0, 2)
    taps = (w_tap * total_count_scale(channels)).astype(bf16)
    strips = jnp.stack([block[:, 0], block[:, -1], block[:, :, 0], block[:, :, -1]], axis=1)
    strips = strips.reshape(per * 4, side, channels)
    ends = (jnp.asarray(end_slot.reshape(-1)), jnp.asarray(end_row.reshape(-1)))

    params = functools.partial(pltpu.CompilerParams, vmem_limit_bytes=LIMIT)
    sems = [pltpu.SemaphoreType.DMA((n - 1,))] * 2
    all_taps, all_pack = pl.pallas_call(
        functools.partial(gather_kernel, n, count),
        out_shape=(
            jax.ShapeDtypeStruct((n, 9, rc, channels), bf16),
            jax.ShapeDtypeStruct((n, count, side, channels), bf16),
        ),
        in_specs=[SMEM, VMEM, VMEM],
        out_specs=(VMEM, VMEM),
        scratch_shapes=[pltpu.VMEM((count, side, channels), bf16)] + sems * 5,
        compiler_params=params(collective_id=0, has_side_effects=True),
    )(index, taps, strips)

    wide = per * side

    def by_row(value):
        return value.transpose(1, 0, 2, 3).reshape(side, wide, channels)

    def by_tile(value):
        return value.reshape(side, per, side, channels).transpose(1, 0, 2, 3)[None]

    tall = (side + 2) * wide
    act, wgrad, kern, dpre = pl.pallas_call(
        functools.partial(main_kernel, n),
        out_shape=(
            jax.ShapeDtypeStruct((side, wide, channels), bf16),
            jax.ShapeDtypeStruct((n, 9, rc, channels), f32),
            jax.ShapeDtypeStruct((9, channels, channels), bf16),
            jax.ShapeDtypeStruct(((side + 4) * wide, channels), bf16),
        ),
        in_specs=[SMEM] * 8 + [VMEM] * 5,
        out_specs=(VMEM,) * 4,
        scratch_shapes=[pltpu.VMEM((channels // LANES, tall, LANES), f32)] * 3
        + [pltpu.VMEM((tall, channels), bf16)] * 3,
        compiler_params=params(),
    )(*tables, *ends, by_row(block), by_row(cotangent[0]), all_taps, all_pack, strips)

    bit = jnp.clip(gossip_bit, 0, levels - 1)
    averaged, all_back, inner, side_grads, corner_grads = pl.pallas_call(
        functools.partial(reduce_kernel, n, count, levels, total_count),
        out_shape=(
            jax.ShapeDtypeStruct((9, rc, channels), f32),
            jax.ShapeDtypeStruct((n, blocks, side, channels), bf16),
            jax.ShapeDtypeStruct((channels // LANES, side * wide, LANES), f32),
            jax.ShapeDtypeStruct((per * 4, side, channels), bf16),
            jax.ShapeDtypeStruct((per // 2, 8, channels), bf16),
        ),
        in_specs=[SMEM, SMEM, VMEM, VMEM, VMEM, VMEM],
        out_specs=(VMEM,) * 5,
        scratch_shapes=[pltpu.VMEM((channels // LANES, tall, LANES), f32)] * 3
        + [
            pltpu.VMEM((blocks, side, channels), bf16),
            pltpu.VMEM((line, 9, rc, channels), jnp.int16),
            pltpu.VMEM((line, 9, 1, channels), f32),
            pltpu.VMEM((line, 9, rc, channels), jnp.int16),
            pltpu.VMEM((line, 9, 1, channels), f32),
            pltpu.VMEM((line - 1, 9, rc, channels), jnp.int16),
            pltpu.VMEM((line - 1, 9, 1, channels), f32),
            pltpu.VMEM((line - 1, 9, rc, channels), jnp.int16),
            pltpu.VMEM((line - 1, 9, 1, channels), f32),
            pltpu.VMEM((n, 8, 128), f32),
            pltpu.VMEM((9, rc, channels), f32),
            pltpu.VMEM((levels, 9, rc, channels), f32),
        ]
        + [pltpu.SemaphoreType.DMA((line,))] * 4
        + [pltpu.SemaphoreType.DMA((line - 1,))] * 4
        + sems
        + [pltpu.SemaphoreType.DMA((levels,))] * 2
        + [pltpu.SemaphoreType.DMA((2, n - 1))] * 2,
        compiler_params=params(collective_id=1, has_side_effects=True),
    )(index, bit, wgrad, kern, dpre, w_tap)

    grads = pl.pallas_call(
        functools.partial(finish_kernel, count),
        out_shape=jax.ShapeDtypeStruct((side, wide, channels), bf16),
        in_specs=[SMEM] * 6 + [VMEM] * 4,
        out_specs=VMEM,
        scratch_shapes=[pltpu.VMEM((channels // LANES, side * wide, LANES), f32)],
        compiler_params=params(),
    )(*tables, inner, all_back, side_grads, corner_grads)

    averaged = averaged.transpose(1, 0, 2).reshape(rows, channels)
    decay = jnp.power(0.99, batch_size[0].astype(f32) / 32.0)
    ema_out = decay * ema[0] + (1.0 - decay) * averaged
    return by_tile(act), by_tile(grads), averaged[None], ema_out[None]


def total_count_scale(channels):
    return (9.0 * channels) ** (-0.5)


def solution(mesh):
    wide = P("rep", "tile", None, None, None)
    thin = P("rep", "tile", None)
    return jax.shard_map(
        body,
        mesh=mesh,
        in_specs=(wide, wide, thin, thin, P(), P(), P(), P(), P(), P()),
        out_specs=(wide, wide, thin, thin),
        check_vma=False,
    )
```

```python
import functools
import math

import jax
import jax.numpy as jnp
import numpy as np
from jax import lax
from jax.experimental import pallas as pl
from jax.experimental.pallas import tpu as pltpu
from jax.sharding import PartitionSpec as P

LEARN = 0.5
MESH = pl.DeviceIdType.MESH
VMEM = pl.BlockSpec(memory_space=pltpu.VMEM)
SMEM = pl.BlockSpec(memory_space=pltpu.SMEM)
LIMIT = 48 * 1024 * 1024
LANES = 128


def strip_lists(tiles, devices, side):
    sub = math.isqrt(tiles // 12)
    per = tiles // devices
    lists = [[] for _ in range(devices)]
    slot = np.full((tiles, 4), -1, np.int32)
    end_slot = np.zeros((tiles, 4), np.int32)
    end_row = np.zeros((tiles, 4), np.int32)

    def split(tile):
        return tile // (sub * sub), tile % (sub * sub) // sub, tile % sub

    def near(tile, down, right):
        face, row, col = split(tile)
        r, c = row + down, col + right
        inside = 0 <= r < sub and 0 <= c < sub
        return inside and (face * sub * sub + r * sub + c) // per == tile // per

    def add(tile, edge):
        found = lists[tile // per]
        slot[tile, edge] = len(found)
        found.append(tile % per * 4 + edge)

    for tile in range(tiles):
        for edge, (down, right) in enumerate(((-1, 0), (1, 0), (0, -1), (0, 1))):
            if not near(tile, down, right):
                add(tile, edge)
    for tile in range(tiles):
        for q in range(4):
            a, b = divmod(q, 2)
            if near(tile, 2 * a - 1, 2 * b - 1):
                continue
            if slot[tile, a] < 0 and slot[tile, 2 + b] < 0:
                add(tile, a)
            if slot[tile, a] >= 0:
                end_slot[tile, q], end_row[tile, q] = slot[tile, a], b * (side - 1)
            else:
                end_slot[tile, q], end_row[tile, q] = slot[tile, 2 + b], a * (side - 1)
    most = max(len(found) for found in lists)
    table = np.zeros((devices, most), np.int32)
    for owner, found in enumerate(lists):
        table[owner, : len(found)] = found
    return most, table, np.maximum(slot, 0), end_slot, end_row


def greet(peers):
    barrier = pltpu.get_barrier_semaphore()
    for peer in peers:
        pl.semaphore_signal(barrier, inc=1, device_id=peer, device_id_type=MESH)
    pl.semaphore_wait(barrier, len(peers))


def tile_peers(n):
    me = lax.axis_index("tile")
    return [{"tile": lax.rem(me + k, n)} for k in range(1, n)]


def send(src, dst, send_sem, recv_sem, peer):
    copy = pltpu.make_async_remote_copy(
        src_ref=src,
        dst_ref=dst,
        send_sem=send_sem,
        recv_sem=recv_sem,
        device_id=peer,
        device_id_type=MESH,
    )
    copy.start()
    return copy


def pack_strips(index, strips, corners, pack, count):
    @pl.loop(0, count)
    def _(k):
        pack[k] = strips[index[k]]

    pack[count:] = corners[...]


class Gather:
    def __init__(self, n, src, dst, rows, sends, recvs):
        self.n, self.dst, self.rows, self.sends, self.recvs = n, dst, rows, sends, recvs
        me = lax.axis_index("tile")
        self.me = me
        self.mate = {"tile": me + 1 - 2 * lax.rem(me, 2)}
        self.first = []
        for k in range(1, n // 2):
            peer = {"tile": lax.rem(me + 2 * k, n)}
            self.first.append(send(src, dst.at[me, rows], sends.at[k - 1], recvs.at[k - 1], peer))
        at = n // 2 - 1
        self.rest = [send(src, dst.at[me, rows], sends.at[at], recvs.at[at], self.mate)]

    def forward(self):
        for k, copy in enumerate(self.first):
            copy.wait_recv()
            block = self.dst.at[lax.rem(self.me + self.n - 2 * (k + 1), self.n), self.rows]
            at = self.n // 2 + k
            self.rest.append(send(block, block, self.sends.at[at], self.recvs.at[at], self.mate))

    def finish(self):
        for copy in self.first:
            copy.wait_send()
        for copy in self.rest:
            copy.wait()


def gather_kernel(n, count, index, taps, strips, all_taps, all_pack, pack, *sems):
    greet(tile_peers(n))
    me = lax.axis_index("tile")
    parts = []
    for c in range(3):
        rows = pl.ds(3 * c, 3)
        parts.append(Gather(n, taps.at[rows], all_taps, rows, *sems[2 * c : 2 * c + 2]))

    @pl.loop(0, count)
    def _(k):
        pack[k] = strips[index[k]]

    cut = count // 2
    for c, rows in enumerate((pl.ds(0, cut), pl.ds(cut, count - cut))):
        parts.append(Gather(n, pack.at[rows], all_pack, rows, *sems[2 * c + 6 : 2 * c + 8]))
    all_taps[me] = taps[...]
    for part in parts:
        part.forward()
    for part in parts:
        part.finish()


STEPS = 32000.0


def encode(value, code, scale):
    top = jnp.maximum(jnp.max(jnp.abs(value), axis=1, keepdims=True), 1e-30)
    code[...] = jnp.round(value * (STEPS / top)).astype(jnp.int32).astype(jnp.int16)
    scale[...] = top * (1.0 / STEPS)


def decode(code, scale):
    return code[...].astype(jnp.int32).astype(jnp.float32) * scale[...]


def put(ref, rows, value):
    for half in range(ref.shape[0]):
        ref[half, rows] = value[:, half * LANES : (half + 1) * LANES]


def get(ref, rows):
    return jnp.concatenate([ref[half, rows] for half in range(ref.shape[0])], axis=1)


def gain(ref, rows, value):
    for half in range(ref.shape[0]):
        ref[half, rows] = ref[half, rows] + value[:, half * LANES : (half + 1) * LANES]


def find_strip(refs, strips, all_pack, t, edge):
    me_ref, links, codes, _, _, slots = refs
    per = strips.shape[0] // 4
    at = t * 4 + edge
    link, code = links[at], codes[at]
    me = me_ref[0]
    owner = link // per
    here = jnp.clip((link - me * per) * 4 + code, 0, per * 4 - 1)
    own = strips[here].astype(jnp.float32)
    other = all_pack[owner, slots[link * 4 + code]].astype(jnp.float32)
    return jnp.where(owner == me, own, other)


def find_end(refs, ends, strips, all_pack, t, q):
    me_ref, _, _, corner_links, corner_codes, _ = refs
    end_slot, end_row = ends
    per, side = strips.shape[0] // 4, strips.shape[1]
    at = t * 4 + q
    link, code = corner_links[at], corner_codes[at]
    me = me_ref[0]
    safe = jnp.maximum(link, 0)
    owner = safe // per
    own = strips[(safe - owner * per) * 4 + code // 2].astype(jnp.float32)
    other = all_pack[owner, end_slot[safe * 4 + code]].astype(jnp.float32)
    rows = jnp.where(owner == me, own, other)
    row = jnp.where(owner == me, lax.rem(code, 2) * (side - 1), end_row[safe * 4 + code])
    chosen = lax.broadcasted_iota(jnp.int32, rows.shape, 0) == row
    chosen = chosen & (link >= 0)
    return jnp.sum(jnp.where(chosen, rows, 0.0), axis=0, keepdims=True)


def find_corner(refs, corners, all_pack, count, t, q):
    me_ref, _, _, corner_links, corner_codes, _ = refs
    per = corners.shape[0] * 2
    at = t * 4 + q
    link, code = corner_links[at], corner_codes[at]
    me = me_ref[0]
    safe = jnp.maximum(link, 0)
    owner = safe // per
    near = safe - owner * per
    own = corners[near // 2].astype(jnp.float32)
    other = all_pack[owner, count + near // 2].astype(jnp.float32)
    rows = jnp.where(owner == me, own, other)
    row = lax.rem(near, 2) * 4 + code
    chosen = lax.broadcasted_iota(jnp.int32, rows.shape, 0) == row
    chosen = chosen & (link >= 0)
    return jnp.sum(jnp.where(chosen, rows, 0.0), axis=0, keepdims=True)


def main_kernel(
    n, me_ref, links, codes, corner_links, corner_codes, slots, end_slot, end_row,
    fields, cot, all_taps, all_pack, strips,
    act, wgrad, kern, dpre,
    e0, e1, e2, x0, x1, x2,
):
    refs = (me_ref, links, codes, corner_links, corner_codes, slots)
    ends = (end_slot, end_row)
    side, wide = fields.shape[0], fields.shape[1]
    per = wide // side
    rc = all_taps.shape[2]
    f32 = jnp.float32
    for owner in range(n):
        for tap in range(9):
            kern[tap, owner * rc : (owner + 1) * rc] = all_taps[owner, tap]
    for i in range(side):
        put(e1, pl.ds((i + 1) * wide, wide), fields[i].astype(f32))

    @pl.loop(0, per)
    def _(t):
        at = pl.multiple_of(t * side, side)
        put(e1, pl.ds(at, side), find_strip(refs, strips, all_pack, t, 0))
        put(e1, pl.ds((side + 1) * wide + at, side), find_strip(refs, strips, all_pack, t, 1))

    for i in range(side + 2):
        rows = pl.ds(i * wide, wide)
        for half in range(e1.shape[0]):
            e0[half, rows] = pltpu.roll(e1[half, rows], 1, 0)
            e2[half, rows] = pltpu.roll(e1[half, rows], wide - 1, 0)

    @pl.loop(0, per)
    def _(t):
        at = t * side
        end = (side + 1) * wide + at
        put(e0, pl.ds(wide + at, side, stride=wide), find_strip(refs, strips, all_pack, t, 2))
        put(e2, pl.ds(wide + at + side - 1, side, stride=wide), find_strip(refs, strips, all_pack, t, 3))
        put(e0, pl.ds(at, 1), find_end(refs, ends, strips, all_pack, t, 0))
        put(e2, pl.ds(at + side - 1, 1), find_end(refs, ends, strips, all_pack, t, 1))
        put(e0, pl.ds(end, 1), find_end(refs, ends, strips, all_pack, t, 2))
        put(e2, pl.ds(end + side - 1, 1), find_end(refs, ends, strips, all_pack, t, 3))

    for x, e in ((x0, e0), (x1, e1), (x2, e2)):
        for half in range(e.shape[0]):
            x[:, half * LANES : (half + 1) * LANES] = e[half].astype(jnp.bfloat16)
    xs = (x0, x1, x2)

    dpre[0 : 2 * wide] = jnp.zeros((2 * wide, dpre.shape[1]), jnp.bfloat16)
    dpre[(side + 2) * wide :] = jnp.zeros((2 * wide, dpre.shape[1]), jnp.bfloat16)

    @pl.loop(0, side)
    def _(i):
        pre = None
        for tap in range(9):
            a, b = divmod(tap, 3)
            rows = xs[b][pl.ds(pl.multiple_of((i + a) * wide, 16), wide)]
            part = jnp.dot(rows, kern[tap], preferred_element_type=f32)
            pre = part if pre is None else pre + part
        s = jax.nn.sigmoid(pre)
        act[i] = (pre * s).astype(jnp.bfloat16)
        grad = cot[i].astype(f32) * (s * (1.0 + pre * (1.0 - s)))
        dpre[pl.ds(pl.multiple_of((i + 2) * wide, 16), wide)] = grad.astype(jnp.bfloat16)

    for tap in range(9):
        a, b = divmod(tap, 3)
        part = lax.dot_general(
            xs[b][a * wide : (a + side) * wide],
            dpre[2 * wide : (side + 2) * wide],
            (((0,), (0,)), ((), ())),
            preferred_element_type=f32,
        )
        for owner in range(n):
            wgrad[owner, tap] = part[owner * rc : (owner + 1) * rc]


def back_field(kern, dpre, inner, side_out, corner_out, d0, d1, d2):
    f32 = jnp.float32
    per, side = side_out.shape[0] // 4, side_out.shape[1]
    wide = per * side

    @pl.loop(0, side + 2)
    def _(i):
        at = pl.multiple_of(i * wide, 16)
        found = []
        for b, d in enumerate((d0, d1, d2)):
            total = None
            for a in range(3):
                rows = dpre[pl.ds(pl.multiple_of((i - a + 2) * wide, 16), wide)]
                part = lax.dot_general(
                    rows, kern[3 * a + b], (((1,), (1,)), ((), ())), preferred_element_type=f32
                )
                total = part if total is None else total + part
            found.append(total)
        put(d0, pl.ds(at, wide), found[0])
        put(d2, pl.ds(at, wide), found[2])
        column = lax.rem(lax.broadcasted_iota(jnp.int32, found[0].shape, 0), side)
        left = jnp.where(column < side - 1, pltpu.roll(found[0], wide - 1, 0), 0.0)
        right = jnp.where(column > 0, pltpu.roll(found[2], 1, 0), 0.0)
        put(d1, pl.ds(at, wide), found[1] + left + right)

    inner[...] = d1[:, wide : (side + 1) * wide]
    last = (side + 1) * wide

    @pl.loop(0, per)
    def _(t):
        at = pl.multiple_of(t * side, side)
        side_out[t * 4] = get(d1, pl.ds(at, side)).astype(jnp.bfloat16)
        side_out[t * 4 + 1] = get(d1, pl.ds(last + at, side)).astype(jnp.bfloat16)
        side_out[t * 4 + 2] = get(d0, pl.ds(wide + at, side, stride=wide)).astype(jnp.bfloat16)
        side_out[t * 4 + 3] = get(d2, pl.ds(wide + at + side - 1, side, stride=wide)).astype(jnp.bfloat16)

    for pair in range(per // 2):
        rows = []
        for t in (2 * pair, 2 * pair + 1):
            at = t * side
            for d, row in ((d0, at), (d2, at + side - 1), (d0, last + at), (d2, last + at + side - 1)):
                rows.append(get(d, pl.ds(row, 1)))
        corner_out[pair] = jnp.concatenate(rows, axis=0).astype(jnp.bfloat16)


def reduce_kernel(
    n, count, levels, total_count, index, bit, wgrad, kern, dpre, weights,
    averaged, all_pack, inner, strips, corners,
    d0, d1, d2, pack, out_y, out_ys, in_y, in_ys, out_z, out_zs, in_z, in_zs, sums, updated, partner,
    s1, r1, s2, r2, s3, r3, s4, r4, s5, r5, s6, r6, s7, r7,
):
    me = lax.axis_index("tile")
    rep = lax.axis_index("rep")
    peers = tile_peers(n)
    friends = []
    for level in range(levels):
        step = 2**level
        friends.append({"rep": rep + step * (1 - 2 * lax.rem(rep // step, 2))})
    greet(peers + friends)
    line = n // 2
    odd = lax.rem(me, 2)
    mate = {"tile": me + 1 - 2 * odd}
    order = list(range(1, line)) + [0]
    near, far = {}, {}
    for k in order:
        there = lax.rem(me - odd + 2 * k, n) + 1 - odd
        encode(wgrad[there], out_y.at[k], out_ys.at[k])
        near[k] = (
            send(out_y.at[k], in_y.at[k], s1.at[k], r1.at[k], mate),
            send(out_ys.at[k], in_ys.at[k], s2.at[k], r2.at[k], mate),
        )
    back_field(kern, dpre, inner, strips, corners, d0, d1, d2)
    grad = None
    for k in order:
        for copy in near[k]:
            copy.wait()
        there = lax.rem(me + 2 * k, n)
        grad = wgrad[there] + decode(in_y.at[k], in_ys.at[k])
        if k > 0:
            encode(grad, out_z.at[k - 1], out_zs.at[k - 1])
            peer = {"tile": there}
            far[k] = (
                send(out_z.at[k - 1], in_z.at[k - 1], s3.at[k - 1], r3.at[k - 1], peer),
                send(out_zs.at[k - 1], in_zs.at[k - 1], s4.at[k - 1], r4.at[k - 1], peer),
            )
    pack_strips(index, strips, corners, pack, count)
    cut = pack.shape[0] // 2
    halo = []
    for c, rows in enumerate((pl.ds(0, cut), pl.ds(cut, pack.shape[0] - cut))):
        halo.append(Gather(n, pack.at[rows], all_pack, rows, s7.at[c], r7.at[c]))
    for k in far:
        for copy in far[k]:
            copy.wait()
        grad = grad + decode(in_z.at[k - 1], in_zs.at[k - 1])
    square = grad * grad
    lanes = sums.shape[2]
    square = jnp.sum(square.reshape(-1, 8, square.shape[2]), axis=0)
    sums[0] = sum(square[:, j : j + lanes] for j in range(0, square.shape[1], lanes))
    small = []
    for k, peer in enumerate(peers):
        small.append(send(sums.at[0], sums.at[k + 1], s5.at[k], r5.at[k], peer))
    halo[0].forward()
    for copy in small:
        copy.wait()
    mean = jnp.sum(sums[...], keepdims=True) / total_count
    updated[...] = weights[...] - LEARN * grad / jnp.sqrt(mean + 1e-06)
    swaps = []
    for level, friend in enumerate(friends):
        swaps.append(send(updated, partner.at[level], s6.at[level], r6.at[level], friend))
    for part in halo[1:]:
        part.forward()
    for copy in swaps:
        copy.wait()
    averaged[...] = 0.5 * (updated[...] + partner[bit[0]])
    for part in halo:
        part.finish()


def finish_kernel(
    count, me_ref, links, codes, corner_links, corner_codes, slots,
    inner, all_pack, strips, corners, out, total,
):
    refs = (me_ref, links, codes, corner_links, corner_codes, slots)
    side, wide = out.shape[0], out.shape[1]
    per = wide // side
    total[...] = inner[...]
    last = (side - 1) * wide

    @pl.loop(0, per)
    def _(t):
        at = pl.multiple_of(t * side, side)
        first = pl.ds(at, side)
        gain(total, first, find_strip(refs, strips, all_pack, t, 0))
        end = pl.ds(last + at, side)
        gain(total, end, find_strip(refs, strips, all_pack, t, 1))
        left = pl.ds(at, side, stride=wide)
        gain(total, left, find_strip(refs, strips, all_pack, t, 2))
        right = pl.ds(at + side - 1, side, stride=wide)
        gain(total, right, find_strip(refs, strips, all_pack, t, 3))
        for q, row in enumerate((at, at + side - 1, last + at, last + at + side - 1)):
            cell = pl.ds(row, 1)
            gain(total, cell, find_corner(refs, corners, all_pack, count, t, q))

    for i in range(side):
        out[i] = get(total, pl.ds(i * wide, wide)).astype(jnp.bfloat16)


def body(
    fields, cotangent, weights, ema, tile_links, tile_codes, corner_links, corner_codes,
    gossip_bit, batch_size,
):
    block = fields[0]
    per, side, _, channels = block.shape
    n = lax.axis_size("tile")
    line = n // 2
    levels = lax.axis_size("rep").bit_length() - 1
    me = lax.axis_index("tile")
    count, table, slot_table, end_slot, end_row = strip_lists(tile_links.shape[0], n, side)
    rows = weights.shape[1]
    rc = rows // 9
    bf16, f32 = jnp.bfloat16, jnp.float32
    total_count = 9.0 * channels * channels
    index = lax.dynamic_slice_in_dim(jnp.asarray(table), me, 1, 0)[0]
    blocks = count + per // 2

    def mine(array):
        return lax.dynamic_slice_in_dim(array, me * per, per, 0).reshape(-1)

    tables = (
        me.astype(jnp.int32).reshape(1),
        mine(tile_links),
        mine(tile_codes),
        mine(corner_links),
        mine(corner_codes),
        jnp.asarray(slot_table.reshape(-1)),
    )
    w_tap = weights[0].reshape(rc, 9, channels).transpose(1, 0, 2)
    taps = (w_tap * total_count_scale(channels)).astype(bf16)
    strips = jnp.stack([block[:, 0], block[:, -1], block[:, :, 0], block[:, :, -1]], axis=1)
    strips = strips.reshape(per * 4, side, channels)
    ends = (jnp.asarray(end_slot.reshape(-1)), jnp.asarray(end_row.reshape(-1)))

    params = functools.partial(pltpu.CompilerParams, vmem_limit_bytes=LIMIT)
    sems = [pltpu.SemaphoreType.DMA((n - 1,))] * 2
    all_taps, all_pack = pl.pallas_call(
        functools.partial(gather_kernel, n, count),
        out_shape=(
            jax.ShapeDtypeStruct((n, 9, rc, channels), bf16),
            jax.ShapeDtypeStruct((n, count, side, channels), bf16),
        ),
        in_specs=[SMEM, VMEM, VMEM],
        out_specs=(VMEM, VMEM),
        scratch_shapes=[pltpu.VMEM((count, side, channels), bf16)] + sems * 5,
        compiler_params=params(collective_id=0, has_side_effects=True),
    )(index, taps, strips)

    wide = per * side

    def by_row(value):
        return value.transpose(1, 0, 2, 3).reshape(side, wide, channels)

    def by_tile(value):
        return value.reshape(side, per, side, channels).transpose(1, 0, 2, 3)[None]

    tall = (side + 2) * wide
    act, wgrad, kern, dpre = pl.pallas_call(
        functools.partial(main_kernel, n),
        out_shape=(
            jax.ShapeDtypeStruct((side, wide, channels), bf16),
            jax.ShapeDtypeStruct((n, 9, rc, channels), f32),
            jax.ShapeDtypeStruct((9, channels, channels), bf16),
            jax.ShapeDtypeStruct(((side + 4) * wide, channels), bf16),
        ),
        in_specs=[SMEM] * 8 + [VMEM] * 5,
        out_specs=(VMEM,) * 4,
        scratch_shapes=[pltpu.VMEM((channels // LANES, tall, LANES), f32)] * 3
        + [pltpu.VMEM((tall, channels), bf16)] * 3,
        compiler_params=params(),
    )(*tables, *ends, by_row(block), by_row(cotangent[0]), all_taps, all_pack, strips)

    bit = jnp.clip(gossip_bit, 0, levels - 1)
    averaged, all_back, inner, side_grads, corner_grads = pl.pallas_call(
        functools.partial(reduce_kernel, n, count, levels, total_count),
        out_shape=(
            jax.ShapeDtypeStruct((9, rc, channels), f32),
            jax.ShapeDtypeStruct((n, blocks, side, channels), bf16),
            jax.ShapeDtypeStruct((channels // LANES, side * wide, LANES), f32),
            jax.ShapeDtypeStruct((per * 4, side, channels), bf16),
            jax.ShapeDtypeStruct((per // 2, 8, channels), bf16),
        ),
        in_specs=[SMEM, SMEM, VMEM, VMEM, VMEM, VMEM],
        out_specs=(VMEM,) * 5,
        scratch_shapes=[pltpu.VMEM((channels // LANES, tall, LANES), f32)] * 3
        + [
            pltpu.VMEM((blocks, side, channels), bf16),
            pltpu.VMEM((line, 9, rc, channels), jnp.int16),
            pltpu.VMEM((line, 9, 1, channels), f32),
            pltpu.VMEM((line, 9, rc, channels), jnp.int16),
            pltpu.VMEM((line, 9, 1, channels), f32),
            pltpu.VMEM((line - 1, 9, rc, channels), jnp.int16),
            pltpu.VMEM((line - 1, 9, 1, channels), f32),
            pltpu.VMEM((line - 1, 9, rc, channels), jnp.int16),
            pltpu.VMEM((line - 1, 9, 1, channels), f32),
            pltpu.VMEM((n, 8, 128), f32),
            pltpu.VMEM((9, rc, channels), f32),
            pltpu.VMEM((levels, 9, rc, channels), f32),
        ]
        + [pltpu.SemaphoreType.DMA((line,))] * 4
        + [pltpu.SemaphoreType.DMA((line - 1,))] * 4
        + sems
        + [pltpu.SemaphoreType.DMA((levels,))] * 2
        + [pltpu.SemaphoreType.DMA((2, n - 1))] * 2,
        compiler_params=params(collective_id=1, has_side_effects=True),
    )(index, bit, wgrad, kern, dpre, w_tap)

    grads = pl.pallas_call(
        functools.partial(finish_kernel, count),
        out_shape=jax.ShapeDtypeStruct((side, wide, channels), bf16),
        in_specs=[SMEM] * 6 + [VMEM] * 4,
        out_specs=VMEM,
        scratch_shapes=[pltpu.VMEM((channels // LANES, side * wide, LANES), f32)],
        compiler_params=params(),
    )(*tables, inner, all_back, side_grads, corner_grads)

    averaged = averaged.transpose(1, 0, 2).reshape(rows, channels)
    decay = jnp.power(0.99, batch_size[0].astype(f32) / 32.0)
    ema_out = decay * ema[0] + (1.0 - decay) * averaged
    return by_tile(act), by_tile(grads), averaged[None], ema_out[None]


def total_count_scale(channels):
    return (9.0 * channels) ** (-0.5)


def solution(mesh):
    wide = P("rep", "tile", None, None, None)
    thin = P("rep", "tile", None)
    return jax.shard_map(
        body,
        mesh=mesh,
        in_specs=(wide, wide, thin, thin, P(), P(), P(), P(), P(), P()),
        out_specs=(wide, wide, thin, thin),
        check_vma=False,
    )
```

```python
import functools
import math

import jax
import jax.numpy as jnp
import numpy as np
from jax import lax
from jax.experimental import pallas as pl
from jax.experimental.pallas import tpu as pltpu
from jax.sharding import PartitionSpec as P

LEARN = 0.5
MESH = pl.DeviceIdType.MESH
VMEM = pl.BlockSpec(memory_space=pltpu.VMEM)
SMEM = pl.BlockSpec(memory_space=pltpu.SMEM)
LIMIT = 48 * 1024 * 1024
LANES = 128


def strip_lists(tiles, devices, side):
    sub = math.isqrt(tiles // 12)
    per = tiles // devices
    lists = [[] for _ in range(devices)]
    slot = np.full((tiles, 4), -1, np.int32)
    end_slot = np.zeros((tiles, 4), np.int32)
    end_row = np.zeros((tiles, 4), np.int32)

    def split(tile):
        return tile // (sub * sub), tile % (sub * sub) // sub, tile % sub

    def near(tile, down, right):
        face, row, col = split(tile)
        r, c = row + down, col + right
        inside = 0 <= r < sub and 0 <= c < sub
        return inside and (face * sub * sub + r * sub + c) // per == tile // per

    def add(tile, edge):
        found = lists[tile // per]
        slot[tile, edge] = len(found)
        found.append(tile % per * 4 + edge)

    for tile in range(tiles):
        for edge, (down, right) in enumerate(((-1, 0), (1, 0), (0, -1), (0, 1))):
            if not near(tile, down, right):
                add(tile, edge)
    for tile in range(tiles):
        for q in range(4):
            a, b = divmod(q, 2)
            if near(tile, 2 * a - 1, 2 * b - 1):
                continue
            if slot[tile, a] < 0 and slot[tile, 2 + b] < 0:
                add(tile, a)
            if slot[tile, a] >= 0:
                end_slot[tile, q], end_row[tile, q] = slot[tile, a], b * (side - 1)
            else:
                end_slot[tile, q], end_row[tile, q] = slot[tile, 2 + b], a * (side - 1)
    most = max(len(found) for found in lists)
    table = np.zeros((devices, most), np.int32)
    for owner, found in enumerate(lists):
        table[owner, : len(found)] = found
    return most, table, np.maximum(slot, 0), end_slot, end_row


def greet(peers):
    barrier = pltpu.get_barrier_semaphore()
    for peer in peers:
        pl.semaphore_signal(barrier, inc=1, device_id=peer, device_id_type=MESH)
    pl.semaphore_wait(barrier, len(peers))


def tile_peers(n):
    me = lax.axis_index("tile")
    return [{"tile": lax.rem(me + k, n)} for k in range(1, n)]


def send(src, dst, send_sem, recv_sem, peer):
    copy = pltpu.make_async_remote_copy(
        src_ref=src,
        dst_ref=dst,
        send_sem=send_sem,
        recv_sem=recv_sem,
        device_id=peer,
        device_id_type=MESH,
    )
    copy.start()
    return copy


def pack_strips(index, strips, corners, pack, count):
    @pl.loop(0, count)
    def _(k):
        pack[k] = strips[index[k]]

    pack[count:] = corners[...]


class Gather:
    def __init__(self, n, src, dst, rows, sends, recvs):
        self.n, self.dst, self.rows, self.sends, self.recvs = n, dst, rows, sends, recvs
        me = lax.axis_index("tile")
        self.me = me
        self.mate = {"tile": me + 1 - 2 * lax.rem(me, 2)}
        self.first = []
        for k in range(1, n // 2):
            peer = {"tile": lax.rem(me + 2 * k, n)}
            self.first.append(send(src, dst.at[me, rows], sends.at[k - 1], recvs.at[k - 1], peer))
        at = n // 2 - 1
        self.rest = [send(src, dst.at[me, rows], sends.at[at], recvs.at[at], self.mate)]

    def forward(self):
        for k, copy in enumerate(self.first):
            copy.wait_recv()
            block = self.dst.at[lax.rem(self.me + self.n - 2 * (k + 1), self.n), self.rows]
            at = self.n // 2 + k
            self.rest.append(send(block, block, self.sends.at[at], self.recvs.at[at], self.mate))

    def finish(self):
        for copy in self.first:
            copy.wait_send()
        for copy in self.rest:
            copy.wait()


def gather_kernel(n, count, index, taps, strips, all_taps, all_pack, pack, *sems):
    greet(tile_peers(n))
    me = lax.axis_index("tile")
    parts = []
    for c in range(3):
        rows = pl.ds(3 * c, 3)
        parts.append(Gather(n, taps.at[rows], all_taps, rows, *sems[2 * c : 2 * c + 2]))

    @pl.loop(0, count)
    def _(k):
        pack[k] = strips[index[k]]

    cut = count // 2
    for c, rows in enumerate((pl.ds(0, cut), pl.ds(cut, count - cut))):
        parts.append(Gather(n, pack.at[rows], all_pack, rows, *sems[2 * c + 6 : 2 * c + 8]))
    all_taps[me] = taps[...]
    for part in parts:
        part.forward()
    for part in parts:
        part.finish()


STEPS = 32000.0


def encode(value, code, scale):
    top = jnp.maximum(jnp.max(jnp.abs(value), axis=1, keepdims=True), 1e-30)
    code[...] = jnp.round(value * (STEPS / top)).astype(jnp.int32).astype(jnp.int16)
    scale[...] = top * (1.0 / STEPS)


def decode(code, scale):
    return code[...].astype(jnp.int32).astype(jnp.float32) * scale[...]


def put(ref, rows, value):
    for half in range(ref.shape[0]):
        ref[half, rows] = value[:, half * LANES : (half + 1) * LANES]


def get(ref, rows):
    return jnp.concatenate([ref[half, rows] for half in range(ref.shape[0])], axis=1)


def gain(ref, rows, value):
    for half in range(ref.shape[0]):
        ref[half, rows] = ref[half, rows] + value[:, half * LANES : (half + 1) * LANES]


def find_strip(refs, strips, all_pack, t, edge):
    me_ref, links, codes, _, _, slots = refs
    per = strips.shape[0] // 4
    at = t * 4 + edge
    link, code = links[at], codes[at]
    me = me_ref[0]
    owner = link // per
    here = jnp.clip((link - me * per) * 4 + code, 0, per * 4 - 1)
    own = strips[here].astype(jnp.float32)
    other = all_pack[owner, slots[link * 4 + code]].astype(jnp.float32)
    return jnp.where(owner == me, own, other)


def find_end(refs, ends, strips, all_pack, t, q):
    me_ref, _, _, corner_links, corner_codes, _ = refs
    end_slot, end_row = ends
    per, side = strips.shape[0] // 4, strips.shape[1]
    at = t * 4 + q
    link, code = corner_links[at], corner_codes[at]
    me = me_ref[0]
    safe = jnp.maximum(link, 0)
    owner = safe // per
    own = strips[(safe - owner * per) * 4 + code // 2].astype(jnp.float32)
    other = all_pack[owner, end_slot[safe * 4 + code]].astype(jnp.float32)
    rows = jnp.where(owner == me, own, other)
    row = jnp.where(owner == me, lax.rem(code, 2) * (side - 1), end_row[safe * 4 + code])
    chosen = lax.broadcasted_iota(jnp.int32, rows.shape, 0) == row
    chosen = chosen & (link >= 0)
    return jnp.sum(jnp.where(chosen, rows, 0.0), axis=0, keepdims=True)


def find_corner(refs, corners, all_pack, count, t, q):
    me_ref, _, _, corner_links, corner_codes, _ = refs
    per = corners.shape[0] * 2
    at = t * 4 + q
    link, code = corner_links[at], corner_codes[at]
    me = me_ref[0]
    safe = jnp.maximum(link, 0)
    owner = safe // per
    near = safe - owner * per
    own = corners[near // 2].astype(jnp.float32)
    other = all_pack[owner, count + near // 2].astype(jnp.float32)
    rows = jnp.where(owner == me, own, other)
    row = lax.rem(near, 2) * 4 + code
    chosen = lax.broadcasted_iota(jnp.int32, rows.shape, 0) == row
    chosen = chosen & (link >= 0)
    return jnp.sum(jnp.where(chosen, rows, 0.0), axis=0, keepdims=True)


def main_kernel(
    n, me_ref, links, codes, corner_links, corner_codes, slots, end_slot, end_row,
    fields, cot, all_taps, all_pack, strips,
    act, inner, side_out, corner_out, dpre, x0, x1, x2,
    e0, e1, e2, kern, d0, d1, d2,
):
    refs = (me_ref, links, codes, corner_links, corner_codes, slots)
    ends = (end_slot, end_row)
    side, wide = fields.shape[0], fields.shape[1]
    per = wide // side
    rc = all_taps.shape[2]
    f32 = jnp.float32
    for owner in range(n):
        for tap in range(9):
            kern[tap, owner * rc : (owner + 1) * rc] = all_taps[owner, tap]
    for i in range(side):
        put(e1, pl.ds((i + 1) * wide, wide), fields[i].astype(f32))

    @pl.loop(0, per)
    def _(t):
        at = pl.multiple_of(t * side, side)
        put(e1, pl.ds(at, side), find_strip(refs, strips, all_pack, t, 0))
        put(e1, pl.ds((side + 1) * wide + at, side), find_strip(refs, strips, all_pack, t, 1))

    for i in range(side + 2):
        rows = pl.ds(i * wide, wide)
        for half in range(e1.shape[0]):
            e0[half, rows] = pltpu.roll(e1[half, rows], 1, 0)
            e2[half, rows] = pltpu.roll(e1[half, rows], wide - 1, 0)

    @pl.loop(0, per)
    def _(t):
        at = t * side
        end = (side + 1) * wide + at
        put(e0, pl.ds(wide + at, side, stride=wide), find_strip(refs, strips, all_pack, t, 2))
        put(e2, pl.ds(wide + at + side - 1, side, stride=wide), find_strip(refs, strips, all_pack, t, 3))
        put(e0, pl.ds(at, 1), find_end(refs, ends, strips, all_pack, t, 0))
        put(e2, pl.ds(at + side - 1, 1), find_end(refs, ends, strips, all_pack, t, 1))
        put(e0, pl.ds(end, 1), find_end(refs, ends, strips, all_pack, t, 2))
        put(e2, pl.ds(end + side - 1, 1), find_end(refs, ends, strips, all_pack, t, 3))

    for x, e in ((x0, e0), (x1, e1), (x2, e2)):
        for half in range(e.shape[0]):
            x[:, half * LANES : (half + 1) * LANES] = e[half].astype(jnp.bfloat16)
    xs = (x0, x1, x2)

    dpre[0 : 2 * wide] = jnp.zeros((2 * wide, dpre.shape[1]), jnp.bfloat16)
    dpre[(side + 2) * wide :] = jnp.zeros((2 * wide, dpre.shape[1]), jnp.bfloat16)

    @pl.loop(0, side)
    def _(i):
        pre = None
        for tap in range(9):
            a, b = divmod(tap, 3)
            rows = xs[b][pl.ds(pl.multiple_of((i + a) * wide, 16), wide)]
            part = jnp.dot(rows, kern[tap], preferred_element_type=f32)
            pre = part if pre is None else pre + part
        s = jax.nn.sigmoid(pre)
        act[i] = (pre * s).astype(jnp.bfloat16)
        grad = cot[i].astype(f32) * (s * (1.0 + pre * (1.0 - s)))
        dpre[pl.ds(pl.multiple_of((i + 2) * wide, 16), wide)] = grad.astype(jnp.bfloat16)

    back_field(kern, dpre, inner, side_out, corner_out, d0, d1, d2)


def back_field(kern, dpre, inner, side_out, corner_out, d0, d1, d2):
    f32 = jnp.float32
    per, side = side_out.shape[0] // 4, side_out.shape[1]
    wide = per * side

    @pl.loop(0, side + 2)
    def _(i):
        at = pl.multiple_of(i * wide, 16)
        found = []
        for b, d in enumerate((d0, d1, d2)):
            total = None
            for a in range(3):
                rows = dpre[pl.ds(pl.multiple_of((i - a + 2) * wide, 16), wide)]
                part = lax.dot_general(
                    rows, kern[3 * a + b], (((1,), (1,)), ((), ())), preferred_element_type=f32
                )
                total = part if total is None else total + part
            found.append(total)
        put(d0, pl.ds(at, wide), found[0])
        put(d2, pl.ds(at, wide), found[2])
        column = lax.rem(lax.broadcasted_iota(jnp.int32, found[0].shape, 0), side)
        left = jnp.where(column < side - 1, pltpu.roll(found[0], wide - 1, 0), 0.0)
        right = jnp.where(column > 0, pltpu.roll(found[2], 1, 0), 0.0)
        put(d1, pl.ds(at, wide), found[1] + left + right)

    inner[...] = d1[:, wide : (side + 1) * wide]
    last = (side + 1) * wide

    @pl.loop(0, per)
    def _(t):
        at = pl.multiple_of(t * side, side)
        side_out[t * 4] = get(d1, pl.ds(at, side)).astype(jnp.bfloat16)
        side_out[t * 4 + 1] = get(d1, pl.ds(last + at, side)).astype(jnp.bfloat16)
        side_out[t * 4 + 2] = get(d0, pl.ds(wide + at, side, stride=wide)).astype(jnp.bfloat16)
        side_out[t * 4 + 3] = get(d2, pl.ds(wide + at + side - 1, side, stride=wide)).astype(jnp.bfloat16)

    for pair in range(per // 2):
        rows = []
        for t in (2 * pair, 2 * pair + 1):
            at = t * side
            for d, row in ((d0, at), (d2, at + side - 1), (d0, last + at), (d2, last + at + side - 1)):
                rows.append(get(d, pl.ds(row, 1)))
        corner_out[pair] = jnp.concatenate(rows, axis=0).astype(jnp.bfloat16)


def kernel_gradient(n, xs, dpre, wgrad):
    f32 = jnp.float32
    rc = wgrad.shape[2]
    wide = (dpre.shape[0] - xs[0].shape[0]) // 2
    side = dpre.shape[0] // wide - 4
    for tap in range(9):
        a, b = divmod(tap, 3)
        part = lax.dot_general(
            xs[b][a * wide : (a + side) * wide],
            dpre[2 * wide : (side + 2) * wide],
            (((0,), (0,)), ((), ())),
            preferred_element_type=f32,
        )
        for owner in range(n):
            wgrad[owner, tap] = part[owner * rc : (owner + 1) * rc]


def reduce_kernel(
    n, count, levels, total_count, index, bit, x0, x1, x2, dpre, strips, corners, weights,
    averaged, all_pack,
    wgrad, pack, out_y, out_ys, in_y, in_ys, out_z, out_zs, in_z, in_zs, sums, updated, partner,
    s1, r1, s2, r2, s3, r3, s4, r4, s5, r5, s6, r6, s7, r7,
):
    me = lax.axis_index("tile")
    rep = lax.axis_index("rep")
    peers = tile_peers(n)
    friends = []
    for level in range(levels):
        step = 2**level
        friends.append({"rep": rep + step * (1 - 2 * lax.rem(rep // step, 2))})
    greet(peers + friends)
    pack_strips(index, strips, corners, pack, count)
    cut = pack.shape[0] // 2
    halo = []
    for c, rows in enumerate((pl.ds(0, cut), pl.ds(cut, pack.shape[0] - cut))):
        halo.append(Gather(n, pack.at[rows], all_pack, rows, s7.at[c], r7.at[c]))
    kernel_gradient(n, (x0, x1, x2), dpre, wgrad)
    line = n // 2
    odd = lax.rem(me, 2)
    mate = {"tile": me + 1 - 2 * odd}
    order = list(range(1, line)) + [0]
    near, far = {}, {}
    for k in order:
        there = lax.rem(me - odd + 2 * k, n) + 1 - odd
        encode(wgrad[there], out_y.at[k], out_ys.at[k])
        near[k] = (
            send(out_y.at[k], in_y.at[k], s1.at[k], r1.at[k], mate),
            send(out_ys.at[k], in_ys.at[k], s2.at[k], r2.at[k], mate),
        )
    grad = None
    for k in order:
        for copy in near[k]:
            copy.wait()
        there = lax.rem(me + 2 * k, n)
        grad = wgrad[there] + decode(in_y.at[k], in_ys.at[k])
        if k > 0:
            encode(grad, out_z.at[k - 1], out_zs.at[k - 1])
            peer = {"tile": there}
            far[k] = (
                send(out_z.at[k - 1], in_z.at[k - 1], s3.at[k - 1], r3.at[k - 1], peer),
                send(out_zs.at[k - 1], in_zs.at[k - 1], s4.at[k - 1], r4.at[k - 1], peer),
            )
    for part in halo:
        part.forward()
    for k in far:
        for copy in far[k]:
            copy.wait()
        grad = grad + decode(in_z.at[k - 1], in_zs.at[k - 1])
    square = grad * grad
    lanes = sums.shape[2]
    square = jnp.sum(square.reshape(-1, 8, square.shape[2]), axis=0)
    sums[0] = sum(square[:, j : j + lanes] for j in range(0, square.shape[1], lanes))
    small = []
    for k, peer in enumerate(peers):
        small.append(send(sums.at[0], sums.at[k + 1], s5.at[k], r5.at[k], peer))
    for copy in small:
        copy.wait()
    mean = jnp.sum(sums[...], keepdims=True) / total_count
    updated[...] = weights[...] - LEARN * grad / jnp.sqrt(mean + 1e-06)
    swaps = []
    for level, friend in enumerate(friends):
        swaps.append(send(updated, partner.at[level], s6.at[level], r6.at[level], friend))
    for copy in swaps:
        copy.wait()
    averaged[...] = 0.5 * (updated[...] + partner[bit[0]])
    for part in halo:
        part.finish()


def finish_kernel(
    count, me_ref, links, codes, corner_links, corner_codes, slots,
    inner, all_pack, strips, corners, out, total,
):
    refs = (me_ref, links, codes, corner_links, corner_codes, slots)
    side, wide = out.shape[0], out.shape[1]
    per = wide // side
    total[...] = inner[...]
    last = (side - 1) * wide

    @pl.loop(0, per)
    def _(t):
        at = pl.multiple_of(t * side, side)
        first = pl.ds(at, side)
        gain(total, first, find_strip(refs, strips, all_pack, t, 0))
        end = pl.ds(last + at, side)
        gain(total, end, find_strip(refs, strips, all_pack, t, 1))
        left = pl.ds(at, side, stride=wide)
        gain(total, left, find_strip(refs, strips, all_pack, t, 2))
        right = pl.ds(at + side - 1, side, stride=wide)
        gain(total, right, find_strip(refs, strips, all_pack, t, 3))
        for q, row in enumerate((at, at + side - 1, last + at, last + at + side - 1)):
            cell = pl.ds(row, 1)
            gain(total, cell, find_corner(refs, corners, all_pack, count, t, q))

    for i in range(side):
        out[i] = get(total, pl.ds(i * wide, wide)).astype(jnp.bfloat16)


def body(
    fields, cotangent, weights, ema, tile_links, tile_codes, corner_links, corner_codes,
    gossip_bit, batch_size,
):
    block = fields[0]
    per, side, _, channels = block.shape
    n = lax.axis_size("tile")
    line = n // 2
    levels = lax.axis_size("rep").bit_length() - 1
    me = lax.axis_index("tile")
    count, table, slot_table, end_slot, end_row = strip_lists(tile_links.shape[0], n, side)
    rows = weights.shape[1]
    rc = rows // 9
    bf16, f32 = jnp.bfloat16, jnp.float32
    total_count = 9.0 * channels * channels
    index = lax.dynamic_slice_in_dim(jnp.asarray(table), me, 1, 0)[0]
    blocks = count + per // 2

    def mine(array):
        return lax.dynamic_slice_in_dim(array, me * per, per, 0).reshape(-1)

    tables = (
        me.astype(jnp.int32).reshape(1),
        mine(tile_links),
        mine(tile_codes),
        mine(corner_links),
        mine(corner_codes),
        jnp.asarray(slot_table.reshape(-1)),
    )
    w_tap = weights[0].reshape(rc, 9, channels).transpose(1, 0, 2)
    taps = (w_tap * total_count_scale(channels)).astype(bf16)
    strips = jnp.stack([block[:, 0], block[:, -1], block[:, :, 0], block[:, :, -1]], axis=1)
    strips = strips.reshape(per * 4, side, channels)
    ends = (jnp.asarray(end_slot.reshape(-1)), jnp.asarray(end_row.reshape(-1)))

    params = functools.partial(pltpu.CompilerParams, vmem_limit_bytes=LIMIT)
    sems = [pltpu.SemaphoreType.DMA((n - 1,))] * 2
    all_taps, all_pack = pl.pallas_call(
        functools.partial(gather_kernel, n, count),
        out_shape=(
            jax.ShapeDtypeStruct((n, 9, rc, channels), bf16),
            jax.ShapeDtypeStruct((n, count, side, channels), bf16),
        ),
        in_specs=[SMEM, VMEM, VMEM],
        out_specs=(VMEM, VMEM),
        scratch_shapes=[pltpu.VMEM((count, side, channels), bf16)] + sems * 5,
        compiler_params=params(collective_id=0, has_side_effects=True),
    )(index, taps, strips)

    wide = per * side

    def by_row(value):
        return value.transpose(1, 0, 2, 3).reshape(side, wide, channels)

    def by_tile(value):
        return value.reshape(side, per, side, channels).transpose(1, 0, 2, 3)[None]

    tall = (side + 2) * wide
    flat = jax.ShapeDtypeStruct((tall, channels), bf16)
    act, inner, side_grads, corner_grads, dpre, x0, x1, x2 = pl.pallas_call(
        functools.partial(main_kernel, n),
        out_shape=(
            jax.ShapeDtypeStruct((side, wide, channels), bf16),
            jax.ShapeDtypeStruct((channels // LANES, side * wide, LANES), f32),
            jax.ShapeDtypeStruct((per * 4, side, channels), bf16),
            jax.ShapeDtypeStruct((per // 2, 8, channels), bf16),
            jax.ShapeDtypeStruct(((side + 4) * wide, channels), bf16),
            flat,
            flat,
            flat,
        ),
        in_specs=[SMEM] * 8 + [VMEM] * 5,
        out_specs=(VMEM,) * 8,
        scratch_shapes=[pltpu.VMEM((channels // LANES, tall, LANES), f32)] * 3
        + [pltpu.VMEM((9, channels, channels), bf16)]
        + [pltpu.VMEM((channels // LANES, tall, LANES), f32)] * 3,
        compiler_params=params(),
    )(*tables, *ends, by_row(block), by_row(cotangent[0]), all_taps, all_pack, strips)

    bit = jnp.clip(gossip_bit, 0, levels - 1)
    averaged, all_back = pl.pallas_call(
        functools.partial(reduce_kernel, n, count, levels, total_count),
        out_shape=(
            jax.ShapeDtypeStruct((9, rc, channels), f32),
            jax.ShapeDtypeStruct((n, blocks, side, channels), bf16),
        ),
        in_specs=[SMEM, SMEM] + [VMEM] * 7,
        out_specs=(VMEM,) * 2,
        scratch_shapes=[
            pltpu.VMEM((n, 9, rc, channels), f32),
            pltpu.VMEM((blocks, side, channels), bf16),
            pltpu.VMEM((line, 9, rc, channels), jnp.int16),
            pltpu.VMEM((line, 9, 1, channels), f32),
            pltpu.VMEM((line, 9, rc, channels), jnp.int16),
            pltpu.VMEM((line, 9, 1, channels), f32),
            pltpu.VMEM((line - 1, 9, rc, channels), jnp.int16),
            pltpu.VMEM((line - 1, 9, 1, channels), f32),
            pltpu.VMEM((line - 1, 9, rc, channels), jnp.int16),
            pltpu.VMEM((line - 1, 9, 1, channels), f32),
            pltpu.VMEM((n, 8, 128), f32),
            pltpu.VMEM((9, rc, channels), f32),
            pltpu.VMEM((levels, 9, rc, channels), f32),
        ]
        + [pltpu.SemaphoreType.DMA((line,))] * 4
        + [pltpu.SemaphoreType.DMA((line - 1,))] * 4
        + sems
        + [pltpu.SemaphoreType.DMA((levels,))] * 2
        + [pltpu.SemaphoreType.DMA((2, n - 1))] * 2,
        compiler_params=params(collective_id=1, has_side_effects=True),
    )(index, bit, x0, x1, x2, dpre, side_grads, corner_grads, w_tap)

    grads = pl.pallas_call(
        functools.partial(finish_kernel, count),
        out_shape=jax.ShapeDtypeStruct((side, wide, channels), bf16),
        in_specs=[SMEM] * 6 + [VMEM] * 4,
        out_specs=VMEM,
        scratch_shapes=[pltpu.VMEM((channels // LANES, side * wide, LANES), f32)],
        compiler_params=params(),
    )(*tables, inner, all_back, side_grads, corner_grads)

    averaged = averaged.transpose(1, 0, 2).reshape(rows, channels)
    decay = jnp.power(0.99, batch_size[0].astype(f32) / 32.0)
    ema_out = decay * ema[0] + (1.0 - decay) * averaged
    return by_tile(act), by_tile(grads), averaged[None], ema_out[None]


def total_count_scale(channels):
    return (9.0 * channels) ** (-0.5)


def solution(mesh):
    wide = P("rep", "tile", None, None, None)
    thin = P("rep", "tile", None)
    return jax.shard_map(
        body,
        mesh=mesh,
        in_specs=(wide, wide, thin, thin, P(), P(), P(), P(), P(), P()),
        out_specs=(wide, wide, thin, thin),
        check_vma=False,
    )
```
